128 devices in a mesh: dp: 2 (over z_lo), cfg: 2 (over core), pipe: 8 (over z_hi, x), seq: 4 (over y).
Axes of the slice: x: 4, y: 4, z: 4 (z_hi: 2, z_lo: 2; z = z_hi * 2 + z_lo), core: 2. Of those that a mesh axis runs over, the one named last changes fastest.
Arguments:
- image_states: bfloat16 [2, 8192, 3072], P('cfg', ('dp', 'pipe', 'seq')), parts along dimension 1, may hold values from -600 to 600
- prompt_states: bfloat16 [2, 512, 3072], P('cfg', ('dp', 'seq')), parts along dimension 1, may hold values from -6 to 6
- stale_kv: bfloat16 [2, 2, 8192, 1536], P('cfg', None, ('dp', 'pipe', 'seq')), parts along dimension 2, may hold values from -140 to 140
- w_image_qkv: bfloat16 [3, 3072, 1536], P(None, None, 'seq'), may hold values from -0.109375 to 0.109375
- w_prompt_kv: bfloat16 [2, 3072, 1536], P(None, None, 'seq'), may hold values from -0.109375 to 0.109375
- w_output: bfloat16 [1536, 3072], P('seq'), may hold values from -0.5 to 0.5
- mod_table: float32 [50, 3, 3072], replicated, may hold values from -4 to 4
- timestep: int32 [2], P('dp'), parts along dimension 0, may hold values from 0 to 49
- guidance: float32 [2], P('dp'), parts along dimension 0, may hold values from 4 to 8
Outputs:
- guided: bfloat16 [8192, 3072], P(('dp', 'pipe', 'seq'), 'cfg'), parts along dimension 0
The draws below stay inside these ranges and needn't reach their ends.
There are 2 independent parts, one for each index of `dp`. The reference program is written for one: setup_inputs(seed, part) draws one part's arguments, and reference() takes and returns one part's arrays. A program takes and returns all parts, laid end to end along the dimension named above; an argument that names none is the same for every part. Nothing has to cross between parts.
All inputs are finite; a program needn't handle non-finite values.
Results may differ from the reference program's by a relative error of at most 0.015.
The reference program's roundings to bfloat16 on the way (of `modulated`, `prompt_norm`, `weights` and `mixed`) count: a program that leaves them out, or rounds other values in their place, can miss the bound.
Values may be sent and summed in bfloat16 or wider, within the bound.
A program may use at most 128 MiB of HBM per device.

```python
import math
import jax
import jax.numpy as jnp
from jax import lax

MODEL_DIM = 3072
HEAD_COUNT = 12
HEAD_DIM = 128
PROMPT_TOKENS = 256
STEP_COUNT = 50
PATCH_TOKENS = 512
IMAGE_TOKENS = 4096
N_PIPE = 8


def draw_image_states(key, part):
    key = jax.random.fold_in(key, 11)
    first, second, third = jax.random.split(key, 3)
    shape = (2, IMAGE_TOKENS, MODEL_DIM)
    row_scale = jnp.exp(jax.random.uniform(second, (2, IMAGE_TOKENS, 1), jnp.float32, 0.0, math.log(10.0)))
    col_scale = jnp.exp(jax.random.uniform(third, (1, 1, MODEL_DIM), jnp.float32, 0.0, math.log(10.0)))
    base = jax.random.truncated_normal(first, -5.0, 5.0, shape, jnp.float32)
    return (base * row_scale * col_scale).astype(jnp.bfloat16)


def draw_stale_kv(key, part):
    key = jax.random.fold_in(key, 23)
    first = jax.random.fold_in(key, 0)
    shape = (2, 2, IMAGE_TOKENS, HEAD_COUNT * HEAD_DIM)
    base = jax.random.truncated_normal(first, -5.0, 5.0, shape, jnp.float32)
    return base.astype(jnp.bfloat16)


def steps_of(rng, shape, cuts, least, top_value):
    def one(dim, parts):
        heights = jax.random.uniform(jax.random.fold_in(jax.random.fold_in(rng, 6), dim), (parts,), jnp.float32, least / len(cuts), top_value / len(cuts))
        return jnp.repeat(jnp.exp(heights), shape[dim] // parts).reshape((-1,) + (1,) * (len(shape) - dim - 1))

    gain = one(*cuts[0])
    for cut in cuts[1:]:
        gain = gain * one(*cut)
    return gain


def centred(stream_key, dims, deviation, limit, cuts=(), kind=jnp.bfloat16):
    array = jax.random.normal(stream_key, dims, jnp.float32) * deviation
    if len(cuts) > 0:
        array = steps_of(stream_key, dims, cuts, -0.22, 0.18) * array
    return jnp.clip(array, min=-limit, max=limit).astype(kind)


def setup_inputs(seed: int = 0, part: int = 0) -> dict:
    streams_of = jax.random.split(jax.random.key(seed), 10)
    own_keys = jax.random.split(jax.random.fold_in(streams_of[9], part), 10)
    image_states = draw_image_states(jax.random.fold_in(jax.random.fold_in(streams_of[9], part), 71), part)
    prompt_states = centred(own_keys[1], (2, PROMPT_TOKENS, MODEL_DIM), 1.0, 6.0, ((0, 2), (1, 4)))
    stale_kv = draw_stale_kv(jax.random.fold_in(jax.random.fold_in(streams_of[9], part), 71), part)
    w_image_qkv = centred(streams_of[3], (3, MODEL_DIM, HEAD_COUNT * HEAD_DIM), MODEL_DIM ** -0.5, 0.109375, ((2, 4),))
    w_prompt_kv = centred(streams_of[4], (2, MODEL_DIM, HEAD_COUNT * HEAD_DIM), MODEL_DIM ** -0.5, 0.109375, ((2, 4),))
    w_output = centred(streams_of[5], (HEAD_COUNT * HEAD_DIM, MODEL_DIM), HEAD_DIM ** -0.5, 0.5, ((0, 4),))
    mod_table = centred(streams_of[6], (STEP_COUNT, 3, MODEL_DIM), 0.7, 4.0, (), jnp.float32)
    timestep = jax.random.randint(own_keys[7], (1,), 0, STEP_COUNT).astype(jnp.int32)
    guidance = jnp.clip(jax.random.uniform(own_keys[8], (1,), jnp.float32, 4.0, 8.0), 4.0, 8.0)
    return {"image_states": image_states, "prompt_states": prompt_states, "stale_kv": stale_kv, "w_image_qkv": w_image_qkv, "w_prompt_kv": w_prompt_kv, "w_output": w_output, "mod_table": mod_table, "timestep": timestep, "guidance": guidance}


def layer_norm(values):
    center = values - lax.optimization_barrier(jnp.mean(values, axis=-1, keepdims=True))
    spread = lax.optimization_barrier(jnp.mean(center * center, axis=-1, keepdims=True))
    return center * lax.rsqrt(spread + 1e-06)

def branch_attention(queries, fresh_keys, fresh_values, stale_keys, stale_values, prompt_keys, prompt_values):
    factor = 1.0 / math.sqrt(HEAD_DIM)
    patch_index = jnp.arange(IMAGE_TOKENS, dtype=jnp.int32) // PATCH_TOKENS

    def one_patch(patch_id):
        is_newer = (patch_index <= patch_id)[:, None]
        key_rows = jnp.concatenate([prompt_keys, jnp.where(is_newer, fresh_keys, stale_keys)], axis=0)
        value_rows = jnp.concatenate([prompt_values, jnp.where(is_newer, fresh_values, stale_values)], axis=0)
        patch_rows = lax.dynamic_slice_in_dim(queries, patch_id * PATCH_TOKENS, PATCH_TOKENS, 0)
        patch_rows = patch_rows.reshape(PATCH_TOKENS, HEAD_COUNT, HEAD_DIM).astype(jnp.float32)
        key_rows = key_rows.reshape(-1, HEAD_COUNT, HEAD_DIM).astype(jnp.float32)
        value_rows = value_rows.reshape(-1, HEAD_COUNT, HEAD_DIM).astype(jnp.float32)
        scores = jnp.einsum('qhd,khd->hqk', patch_rows, key_rows) * factor
        scores = scores - lax.optimization_barrier(jnp.max(scores, axis=-1, keepdims=True))
        weights = jnp.exp(scores)
        weights = (weights / lax.optimization_barrier(jnp.sum(weights, axis=-1, keepdims=True))).astype(jnp.bfloat16)
        weights = lax.optimization_barrier(weights)
        mixture = jnp.einsum('hqk,khd->qhd', weights.astype(jnp.float32), value_rows)
        return mixture.reshape(PATCH_TOKENS, HEAD_COUNT * HEAD_DIM)
    blocks = lax.map(one_patch, jnp.arange(N_PIPE, dtype=jnp.int32))
    return blocks.reshape(IMAGE_TOKENS, HEAD_COUNT * HEAD_DIM)

def reference(image_states, prompt_states, stale_kv, w_image_qkv, w_prompt_kv, w_output, mod_table, timestep, guidance):
    mod_rows = lax.dynamic_index_in_dim(mod_table, timestep[0], 0, keepdims=False)
    attended_list = []
    for branch in range(2):
        modulated = (layer_norm(image_states[branch].astype(jnp.float32)) * (1.0 + mod_rows[1]) + mod_rows[0]).astype(jnp.bfloat16)
        queries = jnp.dot(modulated, w_image_qkv[0], preferred_element_type=jnp.float32).astype(jnp.bfloat16)
        fresh_keys = jnp.dot(modulated, w_image_qkv[1], preferred_element_type=jnp.float32).astype(jnp.bfloat16)
        fresh_values = jnp.dot(modulated, w_image_qkv[2], preferred_element_type=jnp.float32).astype(jnp.bfloat16)
        prompt_norm = layer_norm(prompt_states[branch].astype(jnp.float32)).astype(jnp.bfloat16)
        prompt_keys = jnp.dot(prompt_norm, w_prompt_kv[0], preferred_element_type=jnp.float32).astype(jnp.bfloat16)
        prompt_values = jnp.dot(prompt_norm, w_prompt_kv[1], preferred_element_type=jnp.float32).astype(jnp.bfloat16)
        attended = branch_attention(queries, fresh_keys, fresh_values, stale_kv[branch, 0], stale_kv[branch, 1], prompt_keys, prompt_values)
        attended_list.append(attended.astype(jnp.float32))
    cond_part = attended_list[0]
    uncond = attended_list[1]
    mixed = (uncond + guidance[0] * (cond_part - uncond)).astype(jnp.bfloat16)
    product = jnp.dot(mixed, w_output, preferred_element_type=jnp.float32)
    return (mod_rows[2] * product).astype(jnp.bfloat16)
```

```python
import math

import jax
import jax.numpy as jnp
from jax import lax
from jax.experimental import pallas as pl
from jax.experimental.pallas import tpu as pltpu
from jax.sharding import PartitionSpec as P

MESH = pl.DeviceIdType.MESH
HEAD = 128
BF16 = jnp.bfloat16
F32 = jnp.float32


def normalized(rows):
    center = rows - jnp.mean(rows, axis=-1, keepdims=True)
    spread = jnp.mean(center * center, axis=-1, keepdims=True)
    return center * lax.rsqrt(spread + 1e-06)


def kernel(
    img_in, prm_in, stale_in, wqkv_in, wpr_in, wout_in, table_in, step_in, guide_in,
    out_ref,
    img, table, prm, wqkv, wpr, wout, modbuf, prb, pkv, sbuf, kv, q, acc, top, att, peer, mix, mixall,
    lsem, st_s, st_r, m_s, m_r, mf_s, mf_r, pr_s, pr_r, pk_s, pk_r, w_s, w_r, wf_s, wf_r, ss, rs,
    a_s, a_r, x_s, x_r,
):
    dp, cfg, pipe, seq = (lax.axis_index(name) for name in ("dp", "cfg", "pipe", "seq"))
    x, zh = pipe % 4, pipe // 4
    heads, width = q.shape[0], kv.shape[-1]
    out_half = wout.shape[-1]
    model = img.shape[-1]
    scale = math.log2(math.e) / math.sqrt(HEAD)

    def at_seq(d):
        return (dp, cfg, pipe, (seq + d) % 4)

    def at_x(d):
        return (dp, cfg, zh * 4 + (x + d) % 4, seq)

    at_z = (dp, cfg, (1 - zh) * 4 + x, seq)
    at_core = (dp, 1 - cfg, pipe, seq)

    def remote(src, dst, s, r, device):
        return pltpu.make_async_remote_copy(
            src_ref=src, dst_ref=dst, send_sem=s, recv_sem=r, device_id=device, device_id_type=MESH
        )

    barrier = pltpu.get_barrier_semaphore()
    partners = [at_seq(1), at_seq(3), at_seq(2), at_x(1), at_x(3), at_x(2), at_z, at_core]
    for device in partners:
        pl.semaphore_signal(barrier, inc=1, device_id=device, device_id_type=MESH)

    half_cols = pl.ds(pl.multiple_of(cfg * out_half, 128), out_half)

    def seq_cols(d):
        return pl.ds(pl.multiple_of((seq + d) % 4 * width, 128), width)

    loads = [
        pltpu.make_async_copy(img_in.at[0], img, lsem.at[0]),
        pltpu.make_async_copy(table_in, table, lsem.at[1]),
        pltpu.make_async_copy(prm_in.at[0, pl.ds(pl.multiple_of(x * 16, 16), 16)], prm, lsem.at[2]),
        pltpu.make_async_copy(wqkv_in, wqkv, lsem.at[3]),
        pltpu.make_async_copy(stale_in.at[0, :, :, seq_cols(0)], sbuf.at[seq], lsem.at[4]),
        pltpu.make_async_copy(wpr_in, wpr, lsem.at[5]),
        pltpu.make_async_copy(wout_in.at[:, half_cols], wout.at[seq], lsem.at[6]),
    ]
    for load in loads:
        load.start()

    now = step_in[0]
    loads[0].wait()
    loads[1].wait()

    def modulate(first, count):
        def rows16(i, carry):
            rows = pl.ds(pl.multiple_of(first + i * 16, 16), 16)
            shift, gain = table[now, 0:1, :], table[now, 1:2, :]
            values = normalized(img[rows, :].astype(F32)) * (1.0 + gain) + shift
            modbuf[seq, rows, :] = values.astype(BF16)
            return carry

        lax.fori_loop(0, count // 16, rows16, 0)

    modulate(0, 64)
    pl.semaphore_wait(barrier, len(partners))

    stale_out = [
        remote(stale_in.at[0, :, :, seq_cols(d)], sbuf.at[seq], st_s.at[d - 1], st_r.at[seq], at_seq(d))
        for d in (1, 3, 2)
    ]
    for copy in stale_out:
        copy.start()

    def mod_copy(direction, half):
        part = modbuf.at[seq, pl.ds(half * 64, 64)]
        return remote(part, part, m_s.at[direction, half], m_r.at[direction, half], at_seq(1 if direction == 0 else 3))

    mod_out = [[mod_copy(a, b) for b in range(2)] for a in range(2)]
    mod_out[0][0].start()
    modulate(64, 64)
    mod_out[1][1].start()
    mod_out[0][1].start()
    mod_out[1][0].start()

    def mod_arrival(direction, half):
        part = modbuf.at[(seq + (3 if direction == 0 else 1)) % 4, pl.ds(half * 64, 64)]
        return remote(part, part, m_s.at[direction, half], m_r.at[direction, half], at_seq(1))

    def mod_forward(direction):
        part = modbuf.at[(seq + (3 if direction == 0 else 1)) % 4, pl.ds(direction * 64, 64)]
        return remote(part, part, mf_s.at[direction], mf_r.at[direction], at_seq(1 if direction == 0 else 3))

    def mod_forward_arrival(direction):
        part = modbuf.at[(seq + 2) % 4, pl.ds(direction * 64, 64)]
        return remote(part, part, mf_s.at[direction], mf_r.at[direction], at_seq(1))

    loads[2].wait()
    prb[seq] = normalized(prm[...].astype(F32)).astype(BF16)
    prompt_out = [
        remote(prb.at[seq], prb.at[seq], pr_s.at[d - 1], pr_r.at[seq], at_seq(d)) for d in (1, 3, 2)
    ]
    for copy in prompt_out:
        copy.start()

    def chunk_of(k):
        return (seq + (0, 3, 1, 2)[k]) % 4

    def piece(source, slot, k, lane, device):
        c = chunk_of(k)
        return remote(source, kv.at[slot, c], ss.at[lane, c], rs.at[slot, c], device)

    def own_copies(k, fresh):
        source = kv.at[pipe, chunk_of(k)] if fresh else sbuf.at[chunk_of(k)]
        return (
            (x < 3 if fresh else x == 3, piece(source, pipe, k, 0, at_x(1))),
            (x == 0 if fresh else x > 0, piece(source, pipe, k, 1, at_x(3))),
            (zh == 0 if fresh else zh == 1, piece(source, pipe, k, 2, at_z)),
        )

    def send_own(k, fresh):
        for condition, copy in own_copies(k, fresh):
            pl.when(condition)(copy.start)

    def slot_in(d):
        return zh * 4 + (x + d) % 4

    def slot_far(d):
        return (1 - zh) * 4 + (x + d) % 4

    def landed(slot, k):
        here = kv.at[slot, chunk_of(k)]
        remote(here, here, ss.at[0, 0], rs.at[slot, chunk_of(k)], at_x(1)).wait_recv()

    def pass_on(slot, k, lane, device):
        return piece(kv.at[slot, chunk_of(k)], slot, k, lane, device)

    def any_of(places):
        found = x == places[0]
        for place in places[1:]:
            found = found | (x == place)
        return found

    IN_PLUS = ((1, 2), (0, 2))
    IN_MINUS = ((1, 2), (1, 3))
    FAR_PLUS = ((1, 3), (0, 3))
    FAR_MINUS = ((0, 2), (0, 3))

    def spread_far(k):
        return (pass_on(slot_far(0), k, 3, at_x(1)), pass_on(slot_far(0), k, 4, at_x(3)))

    def forward(which, k):
        places = (IN_PLUS, IN_MINUS, FAR_PLUS, FAR_MINUS)[which][k % 2]
        slot = (slot_in(3), slot_in(1), slot_far(3), slot_far(1))[which]
        return any_of(places), pass_on(slot, k, 5 + which, at_x((1, 3, 1, 3)[which]))

    def serve_z(k):
        landed(slot_far(0), k)
        for copy in spread_far(k):
            copy.start()

    def serve(which, k):
        landed((slot_in(3), slot_in(1), slot_far(3), slot_far(1))[which], k)
        condition, copy = forward(which, k)
        pl.when(condition)(copy.start)

    def when(condition, action, *arguments):
        @pl.when(condition)
        def _():
            action(*arguments)

    def late_one(k):
        when(zh == 1, serve_z, k)
        when(x > 0, serve, 0, k)
        when(x == 3, serve, 1, k)

    def late_two(k):
        when(zh == 1, serve, 2, k)
        when(zh == 1, serve, 3, k)

    def project(k):
        c = chunk_of(k)
        rows = modbuf[c]
        for j in (1, 2):
            kv[pipe, c, j - 1] = jnp.dot(rows, wqkv[j], preferred_element_type=F32).astype(BF16)
        send_own(k, True)
        block = jnp.dot(rows, wqkv[0], preferred_element_type=F32).astype(BF16)
        place = pl.ds(pl.multiple_of(c * 128, 128), 128)
        for h in range(heads):
            q[h, place, :] = block[:, h * HEAD : (h + 1) * HEAD]

    loads[3].wait()
    project(0)

    loads[4].wait()
    for d in (1, 3, 2):
        c = (seq + d) % 4
        remote(sbuf.at[c], sbuf.at[c], st_s.at[0], st_r.at[c], at_seq(1)).wait_recv()
    for k in range(4):
        send_own(k, False)

    mod_arrival(0, 0).wait_recv()
    mod_forward(0).start()
    mod_arrival(1, 1).wait_recv()
    mod_forward(1).start()

    loads[5].wait()
    for d in (1, 3, 2):
        c = (seq + d) % 4
        remote(prb.at[c], prb.at[c], pr_s.at[0], pr_r.at[c], at_seq(1)).wait_recv()
    prompt_rows = prb[...].reshape(64, model)
    for j in range(2):
        pkv[x, j] = jnp.dot(prompt_rows, wpr[j], preferred_element_type=F32).astype(BF16)
    pkv_out = [remote(pkv.at[x], pkv.at[x], pk_s.at[d - 1], pk_r.at[x], at_x(d)) for d in (1, 3, 2)]
    for copy in pkv_out:
        copy.start()

    late_one(0)

    mod_arrival(0, 1).wait_recv()
    project(1)
    late_two(0)
    mod_arrival(1, 0).wait_recv()
    project(2)

    loads[6].wait()
    wout_out = [
        remote(wout.at[seq], wout.at[seq], w_s.at[a], w_r.at[a], at_seq(1 if a == 0 else 3)) for a in range(2)
    ]
    for copy in wout_out:
        copy.start()

    for k in range(4):
        when(zh == 0, serve_z, k)
        when(x == 0, serve, 0, k)
        when(x < 3, serve, 1, k)

    late_one(1)
    for direction in range(2):
        mod_forward_arrival(direction).wait_recv()
    project(3)

    late_two(1)
    late_one(2)
    for k in range(4):
        when(zh == 0, serve, 2, k)
        when(zh == 0, serve, 3, k)

    def attend(keys_of, values_of, first):
        def one_head(h, carry):
            lanes = pl.ds(pl.multiple_of(h * HEAD, HEAD), HEAD)
            keys = keys_of(lanes)
            values = values_of(lanes)
            values = jnp.concatenate([values, jnp.ones_like(values)], axis=1)
            scores = lax.dot_general(q[h], keys, (((1,), (1,)), ((), ())), preferred_element_type=F32)
            peak = jnp.max(scores, axis=1, keepdims=True)
            if first:
                new_top = peak
            else:
                old_top = top[h][:, :1]
                new_top = jnp.maximum(old_top, peak)
            weights = jnp.exp2(scores * scale - new_top * scale).astype(BF16)
            part = jnp.dot(weights, values, preferred_element_type=F32)
            if first:
                acc[h] = part
            else:
                acc[h] = acc[h] * jnp.exp2((old_top - new_top) * scale) + part
            top[h] = jnp.broadcast_to(new_top, top.shape[1:])
            return carry

        lax.fori_loop(0, heads, one_head, 0)

    def attend_slot(slot):
        attend(
            lambda lanes: kv[slot, :, 0, :, lanes].reshape(512, HEAD),
            lambda lanes: kv[slot, :, 1, :, lanes].reshape(512, HEAD),
            False,
        )

    for d in (1, 3, 2):
        c = (x + d) % 4
        remote(pkv.at[c], pkv.at[c], pk_s.at[0], pk_r.at[c], at_x(1)).wait_recv()
    attend(
        lambda lanes: pkv[:, 0, :, lanes].reshape(256, HEAD),
        lambda lanes: pkv[:, 1, :, lanes].reshape(256, HEAD),
        True,
    )
    late_two(2)
    late_one(3)
    attend_slot(pipe)
    late_two(3)
    attend_slot(slot_in(3))
    attend_slot(slot_in(1))
    attend_slot(slot_far(0))

    def wout_arrival(direction):
        part = wout.at[(seq + (3 if direction == 0 else 1)) % 4]
        return remote(part, part, w_s.at[direction], w_r.at[direction], at_seq(1))

    def wout_forward(direction, source):
        part = wout.at[source, pl.ds(direction * (width // 2), width // 2)]
        return remote(part, part, wf_s.at[direction], wf_r.at[direction], at_seq(1 if direction == 0 else 3))

    wout_pass = []
    for direction in range(2):
        wout_arrival(direction).wait_recv()
        copy = wout_forward(direction, (seq + (3 if direction == 0 else 1)) % 4)
        copy.start()
        wout_pass.append(copy)

    attend_slot(slot_far(3))
    attend_slot(slot_far(1))
    for k in range(4):
        landed(slot_in(2), k)
    attend_slot(slot_in(2))
    for k in range(4):
        landed(slot_far(2), k)
    attend_slot(slot_far(2))

    att_out = []
    for h in range(heads):
        block = acc[h]
        att[h] = block[:, :HEAD] / block[:, HEAD : HEAD + 1]
        copy = remote(att.at[h], peer.at[h], a_s.at[h], a_r.at[h], at_core)
        copy.start()
        att_out.append(copy)
    guide = guide_in[0]
    first_side = cfg == 0
    for h in range(heads):
        att_out[h].wait_recv()
        mine, other = att[h], peer[h]
        cond_part = jnp.where(first_side, mine, other)
        uncond = jnp.where(first_side, other, mine)
        mixed = (uncond + guide * (cond_part - uncond)).astype(BF16)
        mix[:, :, h * HEAD : (h + 1) * HEAD] = mixed.reshape(4, 128, HEAD)
    mix_out = [
        remote(mix.at[(seq + d) % 4], mixall.at[seq], x_s.at[d - 1], x_r.at[seq], at_seq(d)) for d in (2, 1, 3)
    ]
    for copy in mix_out:
        copy.start()
    total = jnp.dot(mix[seq], wout[seq], preferred_element_type=F32)
    for direction in range(2):
        wout_forward(direction, (seq + 2) % 4).wait_recv()
    for d in (1, 3, 2):
        c = (seq + d) % 4
        remote(mixall.at[c], mixall.at[c], x_s.at[0], x_r.at[c], at_seq(1)).wait_recv()
        total = total + jnp.dot(mixall[c], wout[c], preferred_element_type=F32)
    out_ref[...] = (table[now, 2:3, half_cols] * total).astype(BF16)

    for copy in stale_out + mod_out[0] + mod_out[1] + prompt_out + pkv_out + wout_out + wout_pass + att_out + mix_out:
        copy.wait_send()
    for direction in range(2):
        mod_forward(direction).wait_send()
    for k in range(4):
        for lane in range(3):
            piece(sbuf.at[chunk_of(k)], pipe, k, lane, at_x(1)).wait_send()
        for copy in spread_far(k):
            copy.wait_send()
        for which in range(4):
            condition, copy = forward(which, k)
            pl.when(condition)(copy.wait_send)


def local(
    image_states, prompt_states, stale_kv, w_image_qkv, w_prompt_kv, w_output, mod_table, timestep, guidance
):
    rows, model = image_states.shape[1:]
    width = w_output.shape[0]
    heads = width // HEAD
    half = w_output.shape[1] // 2
    dma = pltpu.SemaphoreType.DMA
    anywhere = pl.BlockSpec(memory_space=pl.ANY)
    scalar = pl.BlockSpec(memory_space=pltpu.SMEM)
    return pl.pallas_call(
        kernel,
        out_shape=jax.ShapeDtypeStruct((rows, half), BF16),
        in_specs=[anywhere] * 7 + [scalar] * 2,
        out_specs=pl.BlockSpec(memory_space=pltpu.VMEM),
        scratch_shapes=[
            pltpu.VMEM((rows, model), BF16),
            pltpu.VMEM(mod_table.shape, F32),
            pltpu.VMEM((16, model), BF16),
            pltpu.VMEM(w_image_qkv.shape, BF16),
            pltpu.VMEM(w_prompt_kv.shape, BF16),
            pltpu.VMEM((4, width, half), BF16),
            pltpu.VMEM((4, rows, model), BF16),
            pltpu.VMEM((4, 16, model), BF16),
            pltpu.VMEM((4, 2, 64, width), BF16),
            pltpu.VMEM((4, 2, rows, width), BF16),
            pltpu.VMEM((8, 4, 2, rows, width), BF16),
            pltpu.VMEM((heads, 4 * rows, HEAD), BF16),
            pltpu.VMEM((heads, 4 * rows, 2 * HEAD), F32),
            pltpu.VMEM((heads, 4 * rows, HEAD), F32),
            pltpu.VMEM((heads, 4 * rows, HEAD), F32),
            pltpu.VMEM((heads, 4 * rows, HEAD), F32),
            pltpu.VMEM((4, rows, width), BF16),
            pltpu.VMEM((4, rows, width), BF16),
            dma((7,)), dma((3,)), dma((4,)), dma((2, 2)), dma((2, 2)), dma((2,)), dma((2,)),
            dma((3,)), dma((4,)), dma((3,)), dma((4,)), dma((2,)), dma((2,)), dma((2,)), dma((2,)),
            dma((9, 4)), dma((8, 4)), dma((heads,)), dma((heads,)), dma((3,)), dma((4,)),
        ],
        compiler_params=pltpu.CompilerParams(
            collective_id=0, has_side_effects=True, vmem_limit_bytes=58 * 2**20
        ),
        name="guided_attention",
    )(image_states, prompt_states, stale_kv, w_image_qkv, w_prompt_kv, w_output, mod_table, timestep, guidance)


def solution(mesh):
    return jax.shard_map(
        local,
        mesh=mesh,
        in_specs=(
            P("cfg", ("dp", "pipe", "seq"), None),
            P("cfg", ("dp", "seq"), None),
            P("cfg", None, ("dp", "pipe", "seq"), None),
            P(None, None, "seq"),
            P(None, None, "seq"),
            P("seq", None),
            P(),
            P("dp"),
            P("dp"),
        ),
        out_specs=P(("dp", "pipe", "seq"), "cfg"),
        check_vma=False,
    )
```

```python
import math

import jax
import jax.numpy as jnp
from jax import lax
from jax.experimental import pallas as pl
from jax.experimental.pallas import tpu as pltpu
from jax.sharding import PartitionSpec as P

MESH = pl.DeviceIdType.MESH
HEAD = 128
BF16 = jnp.bfloat16
F32 = jnp.float32


def normalized(rows):
    center = rows - jnp.mean(rows, axis=-1, keepdims=True)
    spread = jnp.mean(center * center, axis=-1, keepdims=True)
    return center * lax.rsqrt(spread + 1e-06)


def kernel(
    img_in, prm_in, stale_in, wqkv_in, wpr_in, wout_in, table_in, step_in, guide_in,
    out_ref,
    img, table, prm, wqkv, wpr, wout, modbuf, prb, pkv, sbuf, kv, q, acc, top, att, peer, mix, mixall,
    lsem, st_s, st_r, m_s, m_r, mf_s, mf_r, pr_s, pr_r, pk_s, pk_r, w_s, w_r, wf_s, wf_r, ss, rs,
    a_s, a_r, x_s, x_r,
):
    dp, cfg, pipe, seq = (lax.axis_index(name) for name in ("dp", "cfg", "pipe", "seq"))
    x, zh = pipe % 4, pipe // 4
    heads, width = q.shape[0], kv.shape[-1]
    out_half = wout.shape[-1]
    model = img.shape[-1]
    scale = math.log2(math.e) / math.sqrt(HEAD)

    def at_seq(d):
        return (dp, cfg, pipe, (seq + d) % 4)

    def at_x(d):
        return (dp, cfg, zh * 4 + (x + d) % 4, seq)

    at_z = (dp, cfg, (1 - zh) * 4 + x, seq)
    at_core = (dp, 1 - cfg, pipe, seq)

    def remote(src, dst, s, r, device):
        return pltpu.make_async_remote_copy(
            src_ref=src, dst_ref=dst, send_sem=s, recv_sem=r, device_id=device, device_id_type=MESH
        )

    barrier = pltpu.get_barrier_semaphore()
    partners = [at_seq(1), at_seq(3), at_seq(2), at_x(1), at_x(3), at_x(2), at_z, at_core]
    for device in partners:
        pl.semaphore_signal(barrier, inc=1, device_id=device, device_id_type=MESH)

    half_cols = pl.ds(pl.multiple_of(cfg * out_half, 128), out_half)

    def seq_cols(d):
        return pl.ds(pl.multiple_of((seq + d) % 4 * width, 128), width)

    loads = [
        pltpu.make_async_copy(img_in.at[0], img, lsem.at[0]),
        pltpu.make_async_copy(table_in, table, lsem.at[1]),
        pltpu.make_async_copy(prm_in.at[0, pl.ds(pl.multiple_of(x * 16, 16), 16)], prm, lsem.at[2]),
        pltpu.make_async_copy(wqkv_in, wqkv, lsem.at[3]),
        pltpu.make_async_copy(stale_in.at[0, :, :, seq_cols(0)], sbuf.at[seq], lsem.at[4]),
        pltpu.make_async_copy(wpr_in, wpr, lsem.at[5]),
        pltpu.make_async_copy(wout_in.at[:, half_cols], wout.at[seq], lsem.at[6]),
    ]
    for load in loads:
        load.start()

    now = step_in[0]
    loads[0].wait()
    loads[1].wait()

    def modulate(first, count):
        def rows16(i, carry):
            rows = pl.ds(pl.multiple_of(first + i * 16, 16), 16)
            shift, gain = table[0, pl.ds(now, 1), :], table[1, pl.ds(now, 1), :]
            values = normalized(img[rows, :].astype(F32)) * (1.0 + gain) + shift
            modbuf[0, rows, :] = values.astype(BF16)
            return carry

        lax.fori_loop(0, count // 16, rows16, 0)

    modulate(0, 64)
    pl.semaphore_wait(barrier, len(partners))

    stale_out = [
        remote(stale_in.at[0, :, :, seq_cols(d)], sbuf.at[seq], st_s.at[d - 1], st_r.at[seq], at_seq(d))
        for d in (2, 1, 3)
    ]
    for copy in stale_out:
        copy.start()
    modulate(64, 64)

    def half_rows(half):
        return pl.ds(half * 64, 64)

    def mod_copy(direction, order):
        half = direction if order == 0 else 1 - direction
        source = modbuf.at[0, half_rows(half)]
        target = modbuf.at[1 + order, half_rows(direction)]
        return remote(
            source, target, m_s.at[direction, order], m_r.at[direction, order], at_seq(1 if direction == 0 else 3)
        )

    def mod_forward(direction):
        source = modbuf.at[1, half_rows(direction)]
        target = modbuf.at[3, half_rows(direction)]
        return remote(source, target, mf_s.at[direction], mf_r.at[direction], at_seq(1 if direction == 0 else 3))

    mod_out = [[mod_copy(a, b) for b in range(2)] for a in range(2)]

    def piece(source, slot, k, lane, device):
        return remote(source, kv.at[slot, k], ss.at[lane, k], rs.at[slot, k], device)

    def own_copies(k, fresh):
        source = kv.at[pipe, k] if fresh else sbuf.at[k]
        return (
            (x < 3 if fresh else x == 3, piece(source, pipe, k, 0, at_x(1))),
            (x == 0 if fresh else x > 0, piece(source, pipe, k, 1, at_x(3))),
            (zh == 0 if fresh else zh == 1, piece(source, pipe, k, 2, at_z)),
        )

    def send_own(k, fresh):
        for condition, copy in own_copies(k, fresh):
            pl.when(condition)(copy.start)

    def slot_in(d):
        return zh * 4 + (x + d) % 4

    def slot_far(d):
        return (1 - zh) * 4 + (x + d) % 4

    def landed(slot, k):
        here = kv.at[slot, k]
        remote(here, here, ss.at[0, 0], rs.at[slot, k], at_x(1)).wait_recv()

    def pass_on(slot, k, lane, device):
        return piece(kv.at[slot, k], slot, k, lane, device)

    def any_of(places):
        found = x == places[0]
        for place in places[1:]:
            found = found | (x == place)
        return found

    IN_PLUS = ((1, 2), (0, 2))
    IN_MINUS = ((1, 2), (1, 3))
    FAR_PLUS = ((1, 3), (0, 3))
    FAR_MINUS = ((0, 2), (0, 3))

    def spread_far(k):
        return (pass_on(slot_far(0), k, 3, at_x(1)), pass_on(slot_far(0), k, 4, at_x(3)))

    def forward(which, k):
        places = (IN_PLUS, IN_MINUS, FAR_PLUS, FAR_MINUS)[which][k % 2]
        slot = (slot_in(3), slot_in(1), slot_far(3), slot_far(1))[which]
        return any_of(places), pass_on(slot, k, 5 + which, at_x((1, 3, 1, 3)[which]))

    def serve_z(k):
        landed(slot_far(0), k)
        for copy in spread_far(k):
            copy.start()

    def serve(which, k):
        landed((slot_in(3), slot_in(1), slot_far(3), slot_far(1))[which], k)
        condition, copy = forward(which, k)
        pl.when(condition)(copy.start)

    def when(condition, action, *arguments):
        @pl.when(condition)
        def _():
            action(*arguments)

    def late_one(k):
        when(zh == 1, serve_z, k)
        when(x > 0, serve, 0, k)
        when(x == 3, serve, 1, k)

    def late_two(k):
        when(zh == 1, serve, 2, k)
        when(zh == 1, serve, 3, k)

    def project(k):
        rows = modbuf[k]
        for j in (1, 2):
            kv[pipe, k, j - 1] = jnp.dot(rows, wqkv[j], preferred_element_type=F32).astype(BF16)
        send_own(k, True)
        block = jnp.dot(rows, wqkv[0], preferred_element_type=F32).astype(BF16)
        for h in range(heads):
            q[h, k * 128 : (k + 1) * 128, :] = block[:, h * HEAD : (h + 1) * HEAD]

    def early_far(k):
        when(zh == 0, serve_z, k)

    def early_in(k):
        when(x == 0, serve, 0, k)
        when(x < 3, serve, 1, k)

    def early_far_two(k):
        when(zh == 0, serve, 2, k)
        when(zh == 0, serve, 3, k)

    def mod_arrived(order):
        for direction in range(2):
            mod_out[direction][order].wait_recv()
            if order == 0:
                mod_forward(direction).start()

    for copy in stale_out:
        copy.wait_send()
    for order in range(2):
        for direction in range(2):
            mod_out[direction][order].start()

    loads[3].wait()
    project(0)

    loads[4].wait()
    for d in (1, 3, 2):
        c = (seq + d) % 4
        remote(sbuf.at[c], sbuf.at[c], st_s.at[0], st_r.at[c], at_seq(1)).wait_recv()
    for k in range(4):
        send_own(k, False)

    loads[2].wait()
    prb[seq] = normalized(prm[...].astype(F32)).astype(BF16)

    late_one(0)
    early_far(0)
    mod_arrived(0)
    project(1)
    late_two(0)
    early_far(1)
    early_in(0)
    early_in(1)

    mod_arrived(1)
    prompt_out = [
        remote(prb.at[seq], prb.at[seq], pr_s.at[d - 1], pr_r.at[seq], at_seq(d)) for d in (1, 3, 2)
    ]
    for copy in prompt_out:
        copy.start()
    project(2)

    loads[6].wait()
    wout_out = [
        remote(wout.at[seq], wout.at[seq], w_s.at[a], w_r.at[a], at_seq(1 if a == 0 else 3)) for a in range(2)
    ]
    for copy in wout_out:
        copy.start()

    late_one(1)
    early_far(2)
    early_far(3)
    early_in(2)
    early_in(3)
    early_far_two(0)
    early_far_two(1)
    for direction in range(2):
        mod_forward(direction).wait_recv()
    project(3)
    late_two(1)
    late_one(2)

    loads[5].wait()
    for d in (1, 3, 2):
        c = (seq + d) % 4
        remote(prb.at[c], prb.at[c], pr_s.at[0], pr_r.at[c], at_seq(1)).wait_recv()
    prompt_rows = prb[...].reshape(64, model)
    for j in range(2):
        pkv[x, j] = jnp.dot(prompt_rows, wpr[j], preferred_element_type=F32).astype(BF16)
    pkv_out = [remote(pkv.at[x], pkv.at[x], pk_s.at[d - 1], pk_r.at[x], at_x(d)) for d in (1, 3, 2)]
    for copy in pkv_out:
        copy.start()

    early_far_two(2)
    early_far_two(3)
    late_two(2)
    late_one(3)

    def attend(keys_of, values_of, first):
        def one_head(h, carry):
            lanes = pl.ds(pl.multiple_of(h * HEAD, HEAD), HEAD)
            keys = keys_of(lanes)
            values = values_of(lanes)
            values = jnp.concatenate([values, jnp.ones_like(values)], axis=1)
            scores = lax.dot_general(q[h], keys, (((1,), (1,)), ((), ())), preferred_element_type=F32)
            peak = jnp.max(scores, axis=1, keepdims=True)
            if first:
                new_top = peak
            else:
                old_top = top[h][:, :1]
                new_top = jnp.maximum(old_top, peak)
            weights = jnp.exp2(scores * scale - new_top * scale).astype(BF16)
            part = jnp.dot(weights, values, preferred_element_type=F32)
            if first:
                acc[h] = part
            else:
                acc[h] = acc[h] * jnp.exp2((old_top - new_top) * scale) + part
            top[h] = jnp.broadcast_to(new_top, top.shape[1:])
            return carry

        lax.fori_loop(0, heads, one_head, 0)

    def attend_slot(slot, first=False):
        attend(
            lambda lanes: kv[slot, :, 0, :, lanes].reshape(512, HEAD),
            lambda lanes: kv[slot, :, 1, :, lanes].reshape(512, HEAD),
            first,
        )

    attend_slot(pipe, True)
    late_two(3)
    for d in (1, 3, 2):
        c = (x + d) % 4
        remote(pkv.at[c], pkv.at[c], pk_s.at[0], pk_r.at[c], at_x(1)).wait_recv()
    attend(
        lambda lanes: pkv[:, 0, :, lanes].reshape(256, HEAD),
        lambda lanes: pkv[:, 1, :, lanes].reshape(256, HEAD),
        False,
    )
    attend_slot(slot_in(3))
    attend_slot(slot_in(1))
    attend_slot(slot_far(0))

    def wout_arrival(direction):
        part = wout.at[(seq + (3 if direction == 0 else 1)) % 4]
        return remote(part, part, w_s.at[direction], w_r.at[direction], at_seq(1))

    def wout_forward(direction, source):
        part = wout.at[source, pl.ds(direction * (width // 2), width // 2)]
        return remote(part, part, wf_s.at[direction], wf_r.at[direction], at_seq(1 if direction == 0 else 3))

    wout_pass = []
    for direction in range(2):
        wout_arrival(direction).wait_recv()
        copy = wout_forward(direction, (seq + (3 if direction == 0 else 1)) % 4)
        copy.start()
        wout_pass.append(copy)

    attend_slot(slot_far(3))
    attend_slot(slot_far(1))
    for k in range(4):
        landed(slot_in(2), k)
    attend_slot(slot_in(2))
    for k in range(4):
        landed(slot_far(2), k)
    attend_slot(slot_far(2))

    att_out = []
    for h in range(heads):
        block = acc[h]
        att[h] = block[:, :HEAD] / block[:, HEAD : HEAD + 1]
        copy = remote(att.at[h], peer.at[h], a_s.at[h], a_r.at[h], at_core)
        copy.start()
        att_out.append(copy)
    guide = guide_in[0]
    first_side = cfg == 0
    for h in range(heads):
        att_out[h].wait_recv()
        mine, other = att[h], peer[h]
        cond_part = jnp.where(first_side, mine, other)
        uncond = jnp.where(first_side, other, mine)
        mixed = (uncond + guide * (cond_part - uncond)).astype(BF16)
        mix[:, :, :, h * HEAD : (h + 1) * HEAD] = mixed.reshape(4, 2, 64, HEAD)
    mix_out = [
        remote(mix.at[group, part], mixall.at[seq, half], x_s.at[d - 1, half], x_r.at[seq, half], at_seq(d))
        for d, half, group, part in ((2, 0, 3, 0), (2, 1, 3, 1), (1, 0, 2, 1), (1, 1, 1, 1), (3, 0, 1, 0), (3, 1, 2, 0))
    ]
    for copy in mix_out:
        copy.start()
    total = jnp.dot(mix[0].reshape(128, width), wout[seq], preferred_element_type=F32)
    for direction in range(2):
        wout_forward(direction, (seq + 2) % 4).wait_recv()
    for d in (1, 3, 2):
        c = (seq + d) % 4
        for half in range(2):
            here = mixall.at[c, half]
            remote(here, here, x_s.at[0, 0], x_r.at[c, half], at_seq(1)).wait_recv()
        total = total + jnp.dot(mixall[c].reshape(128, width), wout[c], preferred_element_type=F32)
    out_ref[...] = (table[2, pl.ds(now, 1), half_cols] * total).astype(BF16)

    for copy in mod_out[0] + mod_out[1] + prompt_out + pkv_out + wout_out + wout_pass + att_out + mix_out:
        copy.wait_send()
    for direction in range(2):
        mod_forward(direction).wait_send()
    for k in range(4):
        for lane in range(3):
            piece(sbuf.at[k], pipe, k, lane, at_x(1)).wait_send()
        for copy in spread_far(k):
            copy.wait_send()
        for which in range(4):
            condition, copy = forward(which, k)
            pl.when(condition)(copy.wait_send)


def local(
    image_states, prompt_states, stale_kv, w_image_qkv, w_prompt_kv, w_output, mod_table, timestep, guidance
):
    rows, model = image_states.shape[1:]
    table = jnp.transpose(mod_table, (1, 0, 2))
    width = w_output.shape[0]
    heads = width // HEAD
    half = w_output.shape[1] // 2
    dma = pltpu.SemaphoreType.DMA
    anywhere = pl.BlockSpec(memory_space=pl.ANY)
    scalar = pl.BlockSpec(memory_space=pltpu.SMEM)
    return pl.pallas_call(
        kernel,
        out_shape=jax.ShapeDtypeStruct((rows, half), BF16),
        in_specs=[anywhere] * 7 + [scalar] * 2,
        out_specs=pl.BlockSpec(memory_space=pltpu.VMEM),
        scratch_shapes=[
            pltpu.VMEM((rows, model), BF16),
            pltpu.VMEM(table.shape, F32),
            pltpu.VMEM((16, model), BF16),
            pltpu.VMEM(w_image_qkv.shape, BF16),
            pltpu.VMEM(w_prompt_kv.shape, BF16),
            pltpu.VMEM((4, width, half), BF16),
            pltpu.VMEM((4, rows, model), BF16),
            pltpu.VMEM((4, 16, model), BF16),
            pltpu.VMEM((4, 2, 64, width), BF16),
            pltpu.VMEM((4, 2, rows, width), BF16),
            pltpu.VMEM((8, 4, 2, rows, width), BF16),
            pltpu.VMEM((heads, 4 * rows, HEAD), BF16),
            pltpu.VMEM((heads, 4 * rows, 2 * HEAD), F32),
            pltpu.VMEM((heads, 4 * rows, HEAD), F32),
            pltpu.VMEM((heads, 4 * rows, HEAD), F32),
            pltpu.VMEM((heads, 4 * rows, HEAD), F32),
            pltpu.VMEM((4, 2, rows // 2, width), BF16),
            pltpu.VMEM((4, 2, rows // 2, width), BF16),
            dma((7,)), dma((3,)), dma((4,)), dma((2, 2)), dma((2, 2)), dma((2,)), dma((2,)),
            dma((3,)), dma((4,)), dma((3,)), dma((4,)), dma((2,)), dma((2,)), dma((2,)), dma((2,)),
            dma((9, 4)), dma((8, 4)), dma((heads,)), dma((heads,)), dma((3, 2)), dma((4, 2)),
        ],
        compiler_params=pltpu.CompilerParams(
            collective_id=0, has_side_effects=True, vmem_limit_bytes=58 * 2**20
        ),
        name="guided_attention",
    )(image_states, prompt_states, stale_kv, w_image_qkv, w_prompt_kv, w_output, table, timestep, guidance)


def solution(mesh):
    return jax.shard_map(
        local,
        mesh=mesh,
        in_specs=(
            P("cfg", ("dp", "pipe", "seq"), None),
            P("cfg", ("dp", "seq"), None),
            P("cfg", None, ("dp", "pipe", "seq"), None),
            P(None, None, "seq"),
            P(None, None, "seq"),
            P("seq", None),
            P(),
            P("dp"),
            P("dp"),
        ),
        out_specs=P(("dp", "pipe", "seq"), "cfg"),
        check_vma=False,
    )
```

```python
import math

import jax
import jax.numpy as jnp
from jax import lax
from jax.experimental import pallas as pl
from jax.experimental.pallas import tpu as pltpu
from jax.sharding import PartitionSpec as P

MESH = pl.DeviceIdType.MESH
HEAD = 128
BF16 = jnp.bfloat16
F32 = jnp.float32


PLAN = (
    ((20, 21, 22, 23, 16), (17, 18), (19, 12), (13,), (3,), (14,), (15,), (), (1,), (), ()),
    ((20, 21, 22, 23, 0, 16, 4), (17, 5, 18, 6, 1), (19, 7), (), (2,), (14,), (), (3,), (15,), (), ()),
    ((20, 21, 22, 23, 0, 16, 4), (17, 18, 6), (1, 12, 13), (14,), (), (2, 15), (), (19,), (3,), (), ()),
    ((20, 21, 22, 23, 0, 16), (17, 12, 8, 5), (1, 19, 13, 9, 14), (), (2, 15), (3,), (7,), (18,), (), (), ()),
    ((20, 21, 22, 23, 16, 4), (5, 1, 17, 6), (7, 3, 12, 8, 18), (), (), (), (9, 19), (10, 13, 11), (), (), ()),
    ((20, 21, 22, 23, 16, 0, 4), (8, 5, 6), (9, 17, 2, 18), (), (), (19,), (7, 10), (), (11,), (), ()),
    ((20, 21, 22, 16, 0, 4), (5, 17, 1, 6), (7, 23, 18, 2), (), (), (19,), (3,), (10,), (11,), (), ()),
    ((20, 21, 22, 23, 16), (8, 17, 5), (18,), (9,), (19,), (), (10, 7), (), (), (11,), ()),
)
ATTEND = (
    (0, 4, 1, 5, 2, 3, 6, 7),
    (1, 5, 2, 4, 0, 6, 7, 3),
    (2, 3, 7, 5, 6, 1, 4, 0),
    (3, 4, 2, 0, 7, 6, 1, 5),
    (4, 5, 7, 0, 3, 1, 6, 2),
    (5, 7, 1, 6, 4, 0, 2, 3),
    (6, 7, 2, 5, 3, 1, 4, 0),
    (7, 3, 6, 4, 0, 5, 2, 1),
)


def passes_to(place, whence, k):
    upper, x = divmod(place, 4)
    if not upper:
        x = 3 - x
        whence = (1, 0, 3, 2, 4)[whence]
    far = k in (2, 3)
    ways = {
        0: "+" if x == 2 or (x == 1 and k % 2 == 0) or (x == 0 and k % 2 == 1) else "",
        1: ("-" if x == 1 or (x == 2 and k % 2 == 0) or (x == 3 and k % 2 == 1) else "") + ("z" if x < 3 else ""),
        2: "+" if x != 2 or far else "",
        3: "-" if x == 0 and not far else "",
        4: "+-" if x == 3 else "-",
    }[whence]
    return ways if upper else ways.translate(str.maketrans("+-", "-+"))


def patch_from(place, whence):
    upper, x = divmod(place, 4)
    d = (3, 1, 3, 1, 0)[whence]
    return (upper if whence < 2 else 1 - upper) * 4 + (x + d) % 4


def awaited(place, patch, k):
    return any(patch_from(place, w) == patch and passes_to(place, w, k) for w in range(5))


def normalized(rows):
    center = rows - jnp.mean(rows, axis=-1, keepdims=True)
    spread = jnp.mean(center * center, axis=-1, keepdims=True)
    return center * lax.rsqrt(spread + 1e-06)


def kernel(
    img_in, prm_in, stale_in, wqkv_in, wpr_in, wout_in, table_in, step_in, guide_in,
    out_ref,
    img, table, prm, wqkv, wpr, wout, modbuf, prb, pkv, sbuf, kv, q, acc, top, att, peer, mix, mixall,
    lsem, st_s, st_r, m_s, m_r, mf_s, mf_r, pr_s, pr_r, pk_s, pk_r, w_s, w_r, wf_s, wf_r, ss, rs,
    a_s, a_r, x_s, x_r,
):
    dp, cfg, pipe, seq = (lax.axis_index(name) for name in ("dp", "cfg", "pipe", "seq"))
    x, zh = pipe % 4, pipe // 4
    heads, width = q.shape[0], kv.shape[-1]
    out_half = wout.shape[-1]
    model = img.shape[-1]
    scale = math.log2(math.e) / math.sqrt(HEAD)

    def at_seq(d):
        return (dp, cfg, pipe, (seq + d) % 4)

    def at_x(d):
        return (dp, cfg, zh * 4 + (x + d) % 4, seq)

    at_z = (dp, cfg, (1 - zh) * 4 + x, seq)
    at_core = (dp, 1 - cfg, pipe, seq)

    def remote(src, dst, s, r, device):
        return pltpu.make_async_remote_copy(
            src_ref=src, dst_ref=dst, send_sem=s, recv_sem=r, device_id=device, device_id_type=MESH
        )

    barrier = pltpu.get_barrier_semaphore()
    partners = [at_seq(1), at_seq(3), at_seq(2), at_x(1), at_x(3), at_x(2), at_z, at_core]
    for device in partners:
        pl.semaphore_signal(barrier, inc=1, device_id=device, device_id_type=MESH)

    half_cols = pl.ds(pl.multiple_of(cfg * out_half, 128), out_half)

    def seq_cols(d):
        return pl.ds(pl.multiple_of((seq + d) % 4 * width, 128), width)

    loads = [
        pltpu.make_async_copy(img_in.at[0], img, lsem.at[0]),
        pltpu.make_async_copy(table_in, table, lsem.at[1]),
        pltpu.make_async_copy(prm_in.at[0, pl.ds(pl.multiple_of(x * 16, 16), 16)], prm, lsem.at[2]),
        pltpu.make_async_copy(wqkv_in, wqkv, lsem.at[3]),
        pltpu.make_async_copy(stale_in.at[0, :, :, seq_cols(0)], sbuf.at[seq], lsem.at[4]),
        pltpu.make_async_copy(wpr_in, wpr, lsem.at[5]),
        pltpu.make_async_copy(wout_in.at[:, half_cols], wout.at[seq], lsem.at[6]),
    ]
    for load in loads:
        load.start()

    now = step_in[0]
    loads[0].wait()
    loads[1].wait()

    def modulate(first, count):
        def rows16(i, carry):
            rows = pl.ds(pl.multiple_of(first + i * 16, 16), 16)
            shift, gain = table[0, pl.ds(now, 1), :], table[1, pl.ds(now, 1), :]
            values = normalized(img[rows, :].astype(F32)) * (1.0 + gain) + shift
            modbuf[0, rows, :] = values.astype(BF16)
            return carry

        lax.fori_loop(0, count // 16, rows16, 0)

    modulate(0, 64)
    pl.semaphore_wait(barrier, len(partners))

    stale_out = [
        remote(stale_in.at[0, :, :, seq_cols(d)], sbuf.at[seq], st_s.at[d - 1], st_r.at[seq], at_seq(d))
        for d in (2, 1, 3)
    ]
    for copy in stale_out:
        copy.start()
    modulate(64, 64)

    def half_rows(half):
        return pl.ds(half * 64, 64)

    def mod_copy(direction, order):
        half = direction if order == 0 else 1 - direction
        source = modbuf.at[0, half_rows(half)]
        target = modbuf.at[1 + order, half_rows(direction)]
        return remote(
            source, target, m_s.at[direction, order], m_r.at[direction, order], at_seq(1 if direction == 0 else 3)
        )

    def mod_forward(direction):
        source = modbuf.at[1, half_rows(direction)]
        target = modbuf.at[3, half_rows(direction)]
        return remote(source, target, mf_s.at[direction], mf_r.at[direction], at_seq(1 if direction == 0 else 3))

    mod_out = [[mod_copy(a, b) for b in range(2)] for a in range(2)]

    def piece(source, slot, k, lane, device):
        return remote(source, kv.at[slot, k], ss.at[lane, k], rs.at[slot, k], device)

    def toward(way):
        return {"+": at_x(1), "-": at_x(3), "z": at_z}[way]

    def send_own(k):
        for condition, lane, way in ((x < 3, 0, "+"), (x == 0, 1, "-"), (zh == 0, 2, "z")):
            pl.when(condition)(piece(kv.at[pipe, k], pipe, k, lane, toward(way)).start)

    def send_stale(place, k):
        upper, column = divmod(place, 4)
        ways = (("+", 0),) * (column == 3) + (("-", 1),) * (column > 0) + (("z", 2),) * upper
        for way, lane in ways:
            piece(sbuf.at[k], place, k, lane, toward(way)).start()

    def landed(slot, k):
        here = kv.at[slot, k]
        remote(here, here, ss.at[0, 0], rs.at[slot, k], at_x(1)).wait_recv()

    def passed(place, whence, k):
        slot = patch_from(place, whence)
        for way in passes_to(place, whence, k):
            yield piece(kv.at[slot, k], slot, k, 3 + 3 * whence + "+-z".index(way), toward(way))

    def step(place, code):
        whence, k = divmod(code, 4)
        if whence == 5:
            send_stale(place, k)
            return
        landed(patch_from(place, whence), k)
        for copy in passed(place, whence, k):
            copy.start()

    def steps(index):
        for place in range(8):
            if PLAN[place][index]:
                @pl.when(pipe == place)
                def _():
                    for code in PLAN[place][index]:
                        step(place, code)

    def attend_next(index):
        steps(3 + index)
        slot = 0
        for place in range(8):
            patch = ATTEND[place][index]
            slot = slot + jnp.where(pipe == place, patch, 0)
            rest = [k for k in range(4) if patch != place and not awaited(place, patch, k)]
            if rest:
                @pl.when(pipe == place)
                def _():
                    for k in rest:
                        landed(patch, k)
        attend_slot(slot, index == 0)

    def project(k):
        rows = modbuf[k]
        for j in (1, 2):
            kv[pipe, k, j - 1] = jnp.dot(rows, wqkv[j], preferred_element_type=F32).astype(BF16)
        send_own(k)
        block = jnp.dot(rows, wqkv[0], preferred_element_type=F32).astype(BF16)
        for h in range(heads):
            q[h, k * 128 : (k + 1) * 128, :] = block[:, h * HEAD : (h + 1) * HEAD]

    def late_in(k):
        when(x > 0, serve, 0, k)
        when(x == 3, serve, 1, k)

    def late_far(k):
        when(upper, serve, 4, k)

    def late_far_two(k):
        when(upper, serve, 2, k)
        when(upper, serve, 3, k)

    def early_in(k):
        when(x == 0, serve, 0, k)
        when(x < 3, serve, 1, k)

    def early_far(k):
        when(zh == 0, serve, 4, k)

    def early_far_two(k):
        when(zh == 0, serve, 2, k)
        when(zh == 0, serve, 3, k)

    def mod_arrived(order):
        for direction in range(2):
            mod_out[direction][order].wait_recv()
            if order == 0:
                mod_forward(direction).start()

    def attend(keys_of, values_of, first):
        def one_head(h, carry):
            lanes = pl.ds(pl.multiple_of(h * HEAD, HEAD), HEAD)
            keys = keys_of(lanes)
            values = values_of(lanes)
            values = jnp.concatenate([values, jnp.ones_like(values)], axis=1)
            scores = lax.dot_general(q[h], keys, (((1,), (1,)), ((), ())), preferred_element_type=F32)
            peak = jnp.max(scores, axis=1, keepdims=True)
            if first:
                new_top = peak
            else:
                old_top = top[h][:, :1]
                new_top = jnp.maximum(old_top, peak)
            weights = jnp.exp2(scores * scale - new_top * scale).astype(BF16)
            part = jnp.dot(weights, values, preferred_element_type=F32)
            if first:
                acc[h] = part
            else:
                acc[h] = acc[h] * jnp.exp2((old_top - new_top) * scale) + part
            top[h] = jnp.broadcast_to(new_top, top.shape[1:])
            return carry

        lax.fori_loop(0, heads, one_head, 0)

    def attend_slot(slot, first=False):
        attend(
            lambda lanes: kv[slot, :, 0, :, lanes].reshape(512, HEAD),
            lambda lanes: kv[slot, :, 1, :, lanes].reshape(512, HEAD),
            first,
        )

    def stale_arrived():
        loads[4].wait()
        for d in (1, 3, 2):
            c = (seq + d) % 4
            remote(sbuf.at[c], sbuf.at[c], st_s.at[0], st_r.at[c], at_seq(1)).wait_recv()

    def start_mod():
        for copy in stale_out:
            copy.wait_send()
        for order in range(2):
            for direction in range(2):
                mod_out[direction][order].start()

    prompt_out = [
        remote(prb.at[seq], prb.at[seq], pr_s.at[d - 1], pr_r.at[seq], at_seq(d)) for d in (1, 3, 2)
    ]
    pkv_out = [remote(pkv.at[x], pkv.at[x], pk_s.at[d - 1], pk_r.at[x], at_x(d)) for d in (1, 3, 2)]

    def prompt_rows():
        loads[2].wait()
        prb[seq] = normalized(prm[...].astype(F32)).astype(BF16)

    def prompt_send():
        for copy in prompt_out:
            copy.start()

    def prompt_project():
        loads[5].wait()
        for d in (1, 3, 2):
            c = (seq + d) % 4
            remote(prb.at[c], prb.at[c], pr_s.at[0], pr_r.at[c], at_seq(1)).wait_recv()
        rows = prb[...].reshape(64, model)
        for j in range(2):
            pkv[x, j] = jnp.dot(rows, wpr[j], preferred_element_type=F32).astype(BF16)
        for copy in pkv_out:
            copy.start()

    def prompt_attend():
        for d in (1, 3, 2):
            c = (x + d) % 4
            remote(pkv.at[c], pkv.at[c], pk_s.at[0], pk_r.at[c], at_x(1)).wait_recv()
        attend(
            lambda lanes: pkv[:, 0, :, lanes].reshape(256, HEAD),
            lambda lanes: pkv[:, 1, :, lanes].reshape(256, HEAD),
            False,
        )

    def wout_copy(direction):
        return remote(
            wout.at[seq], wout.at[seq], w_s.at[direction], w_r.at[direction], at_seq(1 if direction == 0 else 3)
        )

    def wout_arrival(direction):
        part = wout.at[(seq + (3 if direction == 0 else 1)) % 4]
        return remote(part, part, w_s.at[direction], w_r.at[direction], at_seq(1))

    def wout_forward(direction, source):
        part = wout.at[source, pl.ds(direction * (width // 2), width // 2)]
        return remote(part, part, wf_s.at[direction], wf_r.at[direction], at_seq(1 if direction == 0 else 3))

    wout_out = [wout_copy(direction) for direction in range(2)]
    wout_pass = [wout_forward(direction, (seq + (3 if direction == 0 else 1)) % 4) for direction in range(2)]

    def wout_send():
        loads[6].wait()
        for copy in wout_out:
            copy.start()

    def wout_serve():
        for direction in range(2):
            wout_arrival(direction).wait_recv()
            wout_pass[direction].start()

    def mod_last():
        for direction in range(2):
            mod_forward(direction).wait_recv()

    loads[3].wait()
    project(0)
    start_mod()
    stale_arrived()
    prompt_rows()
    steps(0)
    mod_arrived(0)
    project(1)
    steps(1)
    mod_arrived(1)
    project(2)
    steps(2)
    mod_last()
    prompt_send()
    project(3)
    wout_send()
    for index in range(8):
        attend_next(index)
        if index == 1:
            prompt_project()
        if index == 5:
            prompt_attend()
        if index == 6:
            wout_serve()

    att_out = []
    for h in range(heads):
        block = acc[h]
        att[h] = block[:, :HEAD] / block[:, HEAD : HEAD + 1]
        copy = remote(att.at[h], peer.at[h], a_s.at[h], a_r.at[h], at_core)
        copy.start()
        att_out.append(copy)
    guide = guide_in[0]
    first_side = cfg == 0
    for h in range(heads):
        att_out[h].wait_recv()
        mine, other = att[h], peer[h]
        cond_part = jnp.where(first_side, mine, other)
        uncond = jnp.where(first_side, other, mine)
        mixed = (uncond + guide * (cond_part - uncond)).astype(BF16)
        mix[:, :, :, h * HEAD : (h + 1) * HEAD] = mixed.reshape(4, 2, 64, HEAD)
    mix_out = [
        remote(mix.at[group, part], mixall.at[seq, half], x_s.at[d - 1, half], x_r.at[seq, half], at_seq(d))
        for d, half, group, part in ((2, 0, 3, 0), (2, 1, 3, 1), (1, 0, 2, 1), (1, 1, 1, 1), (3, 0, 1, 0), (3, 1, 2, 0))
    ]
    for copy in mix_out:
        copy.start()
    total = jnp.dot(mix[0].reshape(128, width), wout[seq], preferred_element_type=F32)
    for direction in range(2):
        wout_forward(direction, (seq + 2) % 4).wait_recv()
    for d in (1, 3, 2):
        c = (seq + d) % 4
        for half in range(2):
            here = mixall.at[c, half]
            remote(here, here, x_s.at[0, 0], x_r.at[c, half], at_seq(1)).wait_recv()
        total = total + jnp.dot(mixall[c].reshape(128, width), wout[c], preferred_element_type=F32)
    out_ref[...] = (table[2, pl.ds(now, 1), half_cols] * total).astype(BF16)

    for copy in mod_out[0] + mod_out[1] + prompt_out + pkv_out + wout_out + wout_pass + att_out + mix_out:
        copy.wait_send()
    for direction in range(2):
        mod_forward(direction).wait_send()
    for k in range(4):
        for lane in range(3):
            piece(sbuf.at[k], pipe, k, lane, at_x(1)).wait_send()
    for place in range(8):
        @pl.when(pipe == place)
        def _():
            for k in range(4):
                for whence in range(5):
                    for copy in passed(place, whence, k):
                        copy.wait_send()


def local(
    image_states, prompt_states, stale_kv, w_image_qkv, w_prompt_kv, w_output, mod_table, timestep, guidance
):
    rows, model = image_states.shape[1:]
    table = jnp.transpose(mod_table, (1, 0, 2))
    width = w_output.shape[0]
    heads = width // HEAD
    half = w_output.shape[1] // 2
    dma = pltpu.SemaphoreType.DMA
    anywhere = pl.BlockSpec(memory_space=pl.ANY)
    scalar = pl.BlockSpec(memory_space=pltpu.SMEM)
    return pl.pallas_call(
        kernel,
        out_shape=jax.ShapeDtypeStruct((rows, half), BF16),
        in_specs=[anywhere] * 7 + [scalar] * 2,
        out_specs=pl.BlockSpec(memory_space=pltpu.VMEM),
        scratch_shapes=[
            pltpu.VMEM((rows, model), BF16),
            pltpu.VMEM(table.shape, F32),
            pltpu.VMEM((16, model), BF16),
            pltpu.VMEM(w_image_qkv.shape, BF16),
            pltpu.VMEM(w_prompt_kv.shape, BF16),
            pltpu.VMEM((4, width, half), BF16),
            pltpu.VMEM((4, rows, model), BF16),
            pltpu.VMEM((4, 16, model), BF16),
            pltpu.VMEM((4, 2, 64, width), BF16),
            pltpu.VMEM((4, 2, rows, width), BF16),
            pltpu.VMEM((8, 4, 2, rows, width), BF16),
            pltpu.VMEM((heads, 4 * rows, HEAD), BF16),
            pltpu.VMEM((heads, 4 * rows, 2 * HEAD), F32),
            pltpu.VMEM((heads, 4 * rows, HEAD), F32),
            pltpu.VMEM((heads, 4 * rows, HEAD), F32),
            pltpu.VMEM((heads, 4 * rows, HEAD), F32),
            pltpu.VMEM((4, 2, rows // 2, width), BF16),
            pltpu.VMEM((4, 2, rows // 2, width), BF16),
            dma((7,)), dma((3,)), dma((4,)), dma((2, 2)), dma((2, 2)), dma((2,)), dma((2,)),
            dma((3,)), dma((4,)), dma((3,)), dma((4,)), dma((2,)), dma((2,)), dma((2,)), dma((2,)),
            dma((18, 4)), dma((8, 4)), dma((heads,)), dma((heads,)), dma((3, 2)), dma((4, 2)),
        ],
        compiler_params=pltpu.CompilerParams(
            collective_id=0, has_side_effects=True, vmem_limit_bytes=58 * 2**20
        ),
        name="guided_attention",
    )(image_states, prompt_states, stale_kv, w_image_qkv, w_prompt_kv, w_output, table, timestep, guidance)


def solution(mesh):
    return jax.shard_map(
        local,
        mesh=mesh,
        in_specs=(
            P("cfg", ("dp", "pipe", "seq"), None),
            P("cfg", ("dp", "seq"), None),
            P("cfg", None, ("dp", "pipe", "seq"), None),
            P(None, None, "seq"),
            P(None, None, "seq"),
            P("seq", None),
            P(),
            P("dp"),
            P("dp"),
        ),
        out_specs=P(("dp", "pipe", "seq"), "cfg"),
        check_vma=False,
    )
```

```python
import math

import jax
import jax.numpy as jnp
from jax import lax
from jax.experimental import pallas as pl
from jax.experimental.pallas import tpu as pltpu
from jax.sharding import PartitionSpec as P

MESH = pl.DeviceIdType.MESH
HEAD = 128
BF16 = jnp.bfloat16
F32 = jnp.float32


PLAN = (
    ((17,), (14, 1, 16, 8), (12, 10), (9,), (15, 11), (18, 19), (3,), (), (13,), (), ()),
    ((20, 16, 5, 0), (18, 6, 14, 1), (19, 4, 15), (), (21, 2, 17), (22, 23, 3), (7,), (), (), (), ()),
    ((21, 22, 16, 4, 20, 0, 18), (17, 1), (14, 12), (19, 2), (23,), (6, 3), (13,), (15,), (), (), ()),
    ((20, 21, 16), (0, 8, 13, 18), (17, 1, 12, 19), (), (22,), (23, 9, 2, 3), (14,), (15,), (), (), ()),
    ((21, 16, 20, 6), (4, 17, 7), (9, 18, 13), (), (22, 8, 23, 19), (5,), (11,), (10,), (12,), (), ()),
    ((20, 22, 0, 6, 23, 8, 7), (17, 5, 9), (21, 2, 18, 16, 19), (), (4,), (10,), (), (11,), (), (), ()),
    ((20, 22, 0, 23, 21, 6), (4, 7, 17, 1), (18, 2), (), (16, 5), (19,), (3,), (10,), (), (11,), ()),
    ((20, 21, 22, 23, 16), (17, 8, 13), (18, 12, 9, 5, 14), (), (19,), (7,), (10,), (15,), (11,), (), ()),
)
ATTEND = (
    (0, 7, 4, 3, 1, 5, 6, 2),
    (1, 5, 0, 2, 6, 4, 3, 7),
    (2, 6, 1, 3, 7, 5, 4, 0),
    (3, 7, 2, 6, 4, 0, 5, 1),
    (4, 0, 5, 7, 3, 1, 2, 6),
    (5, 1, 4, 6, 0, 7, 3, 2),
    (6, 7, 2, 5, 3, 4, 1, 0),
    (7, 3, 4, 6, 0, 5, 2, 1),
)
EARLY = (0, 1, 3, 2, 2, 4, 4, 4)

def passes_to(place, whence, k):
    upper, x = divmod(place, 4)
    if not upper:
        x = 3 - x
        whence = (1, 0, 3, 2, 4)[whence]
    far, near = k in (2, 3), k in (0, 1, 2, 3)
    ways = {
        0: "+" if x == 2 or (x == 1 and k % 2 == 0) or (x == 0 and not near) else "",
        1: ("-" if x == 1 or (x == 2 and near) or (x == 3 and k % 2 == 1) else "") + ("z" if x < 3 else ""),
        2: "+" if x != 2 or far else "",
        3: ("-" if x == 0 and not far else "") + ("z" if x == 3 else ""),
        4: "+-" if x == 3 else "-",
    }[whence]
    return ways if upper else ways.translate(str.maketrans("+-", "-+"))


def patch_from(place, whence):
    upper, x = divmod(place, 4)
    d = (3, 1, 3, 1, 0)[whence]
    return (upper if whence < 2 else 1 - upper) * 4 + (x + d) % 4


def awaited(place, patch, k):
    return any(patch_from(place, w) == patch and passes_to(place, w, k) for w in range(5))


def normalized(rows):
    center = rows - jnp.mean(rows, axis=-1, keepdims=True)
    spread = jnp.mean(center * center, axis=-1, keepdims=True)
    return center * lax.rsqrt(spread + 1e-06)


def kernel(
    img_in, prm_in, stale_in, wqkv_in, wpr_in, wout_in, table_in, step_in, guide_in,
    out_ref,
    img, table, prm, wqkv, wpr, wout, modbuf, prb, pkv, sbuf, kv, q, acc, top, att, peer, mix, mixall,
    lsem, st_s, st_r, m_s, m_r, mf_s, mf_r, pr_s, pr_r, pk_s, pk_r, w_s, w_r, wf_s, wf_r, ss, rs, v_s, v_r, u_s, u_r,
    a_s, a_r, x_s, x_r,
):
    dp, cfg, pipe, seq = (lax.axis_index(name) for name in ("dp", "cfg", "pipe", "seq"))
    x, zh = pipe % 4, pipe // 4
    heads, width = q.shape[0], kv.shape[-1]
    out_half = wout.shape[-1]
    model = img.shape[-1]
    scale = math.log2(math.e) / math.sqrt(HEAD)

    def at_seq(d):
        return (dp, cfg, pipe, (seq + d) % 4)

    def at_x(d):
        return (dp, cfg, zh * 4 + (x + d) % 4, seq)

    at_z = (dp, cfg, (1 - zh) * 4 + x, seq)
    at_core = (dp, 1 - cfg, pipe, seq)
    line = zh * 2 + dp
    at_line = [(1 - dp, cfg, pipe, seq), at_z, (1 - dp, cfg, (1 - zh) * 4 + x, seq)]
    line_of = [zh * 2 + 1 - dp, (1 - zh) * 2 + dp, (1 - zh) * 2 + 1 - dp]

    def remote(src, dst, s, r, device):
        return pltpu.make_async_remote_copy(
            src_ref=src, dst_ref=dst, send_sem=s, recv_sem=r, device_id=device, device_id_type=MESH
        )

    barrier = pltpu.get_barrier_semaphore()
    partners = [at_seq(1), at_seq(3), at_seq(2), at_x(1), at_x(3), at_x(2), at_core] + at_line
    for device in partners:
        pl.semaphore_signal(barrier, inc=1, device_id=device, device_id_type=MESH)

    half_cols = pl.ds(pl.multiple_of(cfg * out_half, 128), out_half)

    def seq_cols(d):
        return pl.ds(pl.multiple_of((seq + d) % 4 * width, 128), width)

    def stale_part(k, source):
        return sbuf.at[k, :, pl.ds(pl.multiple_of(source * 32, 32), 32)]

    loads = [
        pltpu.make_async_copy(img_in.at[0], img, lsem.at[0]),
        pltpu.make_async_copy(table_in, table, lsem.at[1]),
        pltpu.make_async_copy(prm_in.at[0, pl.ds(pl.multiple_of(x * 16, 16), 16)], prm, lsem.at[2]),
        pltpu.make_async_copy(wqkv_in, wqkv, lsem.at[3]),
        pltpu.make_async_copy(stale_in.at[0, :, pl.ds(0, 32), seq_cols(0)], stale_part(0, seq), lsem.at[4]),
        pltpu.make_async_copy(wpr_in, wpr, lsem.at[5]),
        pltpu.make_async_copy(wout_in.at[:, half_cols], wout.at[seq], lsem.at[6]),
    ] + [
        pltpu.make_async_copy(
            stale_in.at[0, :, pl.ds(k * 32, 32), seq_cols(0)], stale_part(k, seq), lsem.at[6 + k]
        )
        for k in (1, 2, 3)
    ]
    for load in loads:
        load.start()

    now = step_in[0]
    loads[0].wait()
    loads[1].wait()

    def modulate(first, count):
        def rows16(i, carry):
            rows = pl.ds(pl.multiple_of(first + i * 16, 16), 16)
            shift, gain = table[0, pl.ds(now, 1), :], table[1, pl.ds(now, 1), :]
            values = normalized(img[rows, :].astype(F32)) * (1.0 + gain) + shift
            modbuf[0, rows, :] = values.astype(BF16)
            return carry

        lax.fori_loop(0, count // 16, rows16, 0)

    modulate(0, 64)
    pl.semaphore_wait(barrier, len(partners))

    def any_of(places):
        found = pipe == places[0]
        for place in places[1:]:
            found = found | (pipe == place)
        return found

    def stale_copy(k, d, source):
        return remote(
            stale_in.at[0, :, pl.ds(k * 32, 32), seq_cols(d)], stale_part(k, source),
            st_s.at[d - 1, k], st_r.at[source, k], at_seq(d),
        )

    stale_out = [[stale_copy(k, d, seq) for d in (2, 1, 3)] for k in range(4)]
    early = [[place for place in range(1, 8) if EARLY[place] > k] for k in range(4)]
    late = [[place for place in range(1, 8) if EARLY[place] <= k] for k in range(4)]

    def each_stale(places, act):
        for k in range(4):
            if places[k]:
                @pl.when(any_of(places[k]))
                def _():
                    for copy in stale_out[k]:
                        act(copy)

    each_stale(early, lambda copy: copy.start())
    modulate(64, 64)

    def half_rows(half):
        return pl.ds(half * 64, 64)

    def mod_copy(direction, order):
        half = direction if order == 0 else 1 - direction
        source = modbuf.at[0, half_rows(half)]
        target = modbuf.at[1 + order, half_rows(direction)]
        return remote(
            source, target, m_s.at[direction, order], m_r.at[direction, order], at_seq(1 if direction == 0 else 3)
        )

    def mod_forward(direction):
        source = modbuf.at[1, half_rows(direction)]
        target = modbuf.at[3, half_rows(direction)]
        return remote(source, target, mf_s.at[direction], mf_r.at[direction], at_seq(1 if direction == 0 else 3))

    mod_out = [[mod_copy(a, b) for b in range(2)] for a in range(2)]

    def piece(source, slot, k, lane, device):
        return remote(source, kv.at[slot, k], ss.at[lane, k], rs.at[slot, k], device)

    att_out = [remote(att.at[h], peer.at[h], a_s.at[h], a_r.at[h], at_core) for h in range(heads)]

    def send_attended(h):
        block = acc[h]
        att[h] = block[:, :HEAD] / block[:, HEAD : HEAD + 1]
        att_out[h].start()

    def toward(way):
        return {"+": at_x(1), "-": at_x(3), "z": at_z}[way]

    def send_own(k):
        for condition, lane, way in ((x < 3, 0, "+"), (pipe == 4, 1, "-"), (zh == 0, 2, "z")):
            pl.when(condition)(piece(kv.at[pipe, k], pipe, k, lane, toward(way)).start)

    def send_stale(place, k):
        upper, column = divmod(place, 4)
        for d in (1, 3, 2):
            stale_copy(k, d, (seq + d) % 4).wait_recv()
        ways = (("+", 0),) * (place == 3) + (("-", 1),) * (column > 0) + (("z", 2),) * upper
        for way, lane in ways:
            piece(sbuf.at[k], place, k, lane, toward(way)).start()

    def landed(slot, k):
        here = kv.at[slot, k]
        remote(here, here, ss.at[0, 0], rs.at[slot, k], at_x(1)).wait_recv()

    def passed(place, whence, k):
        slot = patch_from(place, whence)
        for way in passes_to(place, whence, k):
            yield piece(kv.at[slot, k], slot, k, 3 + 3 * whence + "+-z".index(way), toward(way))

    def step(place, code):
        whence, k = divmod(code, 4)
        if whence == 5:
            send_stale(place, k)
            return
        landed(patch_from(place, whence), k)
        for copy in passed(place, whence, k):
            copy.start()

    def steps(index):
        for place in range(8):
            if PLAN[place][index]:
                @pl.when(pipe == place)
                def _():
                    for code in PLAN[place][index]:
                        step(place, code)

    def attend_next(index):
        steps(3 + index)
        slot = 0
        for place in range(8):
            patch = ATTEND[place][index]
            slot = slot + jnp.where(pipe == place, patch, 0)
            rest = [k for k in range(4) if patch != place and not awaited(place, patch, k)]
            if rest:
                @pl.when(pipe == place)
                def _():
                    for k in rest:
                        landed(patch, k)
        attend_slot(slot, index == 0, send_attended if index == 7 else None)

    def project(k):
        rows = modbuf[k]
        for j in (1, 2):
            kv[pipe, k, j - 1] = jnp.dot(rows, wqkv[j], preferred_element_type=F32).astype(BF16)
        send_own(k)
        block = jnp.dot(rows, wqkv[0], preferred_element_type=F32).astype(BF16)
        for h in range(heads):
            q[h, k * 128 : (k + 1) * 128, :] = block[:, h * HEAD : (h + 1) * HEAD]

    def late_in(k):
        when(x > 0, serve, 0, k)
        when(x == 3, serve, 1, k)

    def late_far(k):
        when(upper, serve, 4, k)

    def late_far_two(k):
        when(upper, serve, 2, k)
        when(upper, serve, 3, k)

    def early_in(k):
        when(x == 0, serve, 0, k)
        when(x < 3, serve, 1, k)

    def early_far(k):
        when(zh == 0, serve, 4, k)

    def early_far_two(k):
        when(zh == 0, serve, 2, k)
        when(zh == 0, serve, 3, k)

    def mod_arrived(order):
        for direction in range(2):
            mod_out[direction][order].wait_recv()
            if order == 0:
                mod_forward(direction).start()

    def attend_head(h, keys, values, first):
        values = jnp.concatenate([values, jnp.ones_like(values)], axis=1)
        scores = lax.dot_general(q[h], keys, (((1,), (1,)), ((), ())), preferred_element_type=F32)
        peak = jnp.max(scores, axis=1, keepdims=True)
        if first:
            new_top = peak
        else:
            old_top = top[h][:, :1]
            new_top = jnp.maximum(old_top, peak)
        weights = jnp.exp2(scores * scale - new_top * scale).astype(BF16)
        part = jnp.dot(weights, values, preferred_element_type=F32)
        if first:
            acc[h] = part
        else:
            acc[h] = acc[h] * jnp.exp2((old_top - new_top) * scale) + part
        top[h] = jnp.broadcast_to(new_top, top.shape[1:])

    def attend(keys_of, values_of, first, finish=None):
        for h in range(heads):
            lanes = pl.ds(h * HEAD, HEAD)
            attend_head(h, keys_of(lanes), values_of(lanes), first)
            if finish is not None:
                finish(h)


    def attend_slot(slot, first=False, finish=None):
        attend(
            lambda lanes: kv[slot, :, 0, :, lanes].reshape(512, HEAD),
            lambda lanes: kv[slot, :, 1, :, lanes].reshape(512, HEAD),
            first,
            finish,
        )

    def start_mod():
        for order in range(2):
            for direction in range(2):
                mod_out[direction][order].start()

    prompt_out = [
        remote(prb.at[seq], prb.at[seq], pr_s.at[d - 1], pr_r.at[seq], at_seq(d)) for d in (1, 3, 2)
    ]
    pkv_out = [remote(pkv.at[x], pkv.at[x], pk_s.at[d - 1], pk_r.at[x], at_x(d)) for d in (1, 3, 2)]

    def prompt_rows():
        loads[2].wait()
        prb[seq] = normalized(prm[...].astype(F32)).astype(BF16)

    def prompt_send():
        for copy in prompt_out:
            copy.start()

    def prompt_project():
        loads[5].wait()
        for d in (1, 3, 2):
            c = (seq + d) % 4
            remote(prb.at[c], prb.at[c], pr_s.at[0], pr_r.at[c], at_seq(1)).wait_recv()
        rows = prb[...].reshape(64, model)
        for j in range(2):
            pkv[x, j] = jnp.dot(rows, wpr[j], preferred_element_type=F32).astype(BF16)
        for copy in pkv_out:
            copy.start()

    def prompt_attend():
        for d in (1, 3, 2):
            c = (x + d) % 4
            remote(pkv.at[c], pkv.at[c], pk_s.at[0], pk_r.at[c], at_x(1)).wait_recv()
        attend(
            lambda lanes: pkv[:, 0, :, lanes].reshape(256, HEAD),
            lambda lanes: pkv[:, 1, :, lanes].reshape(256, HEAD),
            False,
        )

    share = out_half // 3
    quarter = width // 4

    def wout_copy(direction):
        part = wout.at[seq, :, pl.ds(0, out_half - share)]
        return remote(part, part, w_s.at[direction], w_r.at[direction], at_seq(1 if direction == 0 else 3))

    def wout_arrival(direction):
        part = wout.at[(seq + (3 if direction == 0 else 1)) % 4, :, pl.ds(0, out_half - share)]
        return remote(part, part, w_s.at[direction], w_r.at[direction], at_seq(1))

    def wout_forward(direction, source):
        part = wout.at[source, pl.ds(direction * (width // 2), width // 2), pl.ds(0, out_half - share)]
        return remote(part, part, wf_s.at[direction], wf_r.at[direction], at_seq(1 if direction == 0 else 3))

    def wout_quarter(source, place):
        rows = pl.ds(pl.multiple_of(place * quarter, 16), quarter)
        return wout.at[source, rows, pl.ds(out_half - share, share)]

    def quarter_copy(source, d):
        part = wout_quarter(source, line)
        return remote(part, part, v_s.at[d - 1], v_r.at[source], at_seq(d))

    def quarter_pass(d, to):
        source = (seq + d) % 4
        part = wout_quarter(source, line)
        return remote(part, part, u_s.at[d - 1, to], u_r.at[source, line], at_line[to])

    def quarter_arrival(d, place):
        source = (seq + d) % 4
        part = wout_quarter(source, place)
        return remote(part, part, u_s.at[0, 0], u_r.at[source, place], at_line[0])

    wout_out = [wout_copy(direction) for direction in range(2)]
    wout_pass = [wout_forward(direction, (seq + (3 if direction == 0 else 1)) % 4) for direction in range(2)]
    quarter_out = [quarter_copy(seq, d) for d in (2, 1, 3)]
    quarter_on = [[quarter_pass(d, to) for to in range(3)] for d in (1, 3, 2)]

    def wout_send():
        loads[6].wait()
        for copy in quarter_out + wout_out:
            copy.start()

    def quarter_serve():
        for d, copies in zip((1, 3, 2), quarter_on):
            quarter_copy((seq + d) % 4, 1).wait_recv()
            for copy in copies:
                copy.start()

    def wout_serve():
        for direction in range(2):
            wout_arrival(direction).wait_recv()
            wout_pass[direction].start()

    def wout_last():
        for direction in range(2):
            wout_forward(direction, (seq + 2) % 4).wait_recv()
        for d in (1, 3, 2):
            for place in line_of:
                quarter_arrival(d, place).wait_recv()

    def mod_last():
        for direction in range(2):
            mod_forward(direction).wait_recv()

    start_mod()
    loads[3].wait()
    project(0)
    for load in [loads[4]] + loads[7:]:
        load.wait()
    prompt_rows()
    steps(0)
    mod_arrived(0)
    each_stale(late, lambda copy: copy.start())
    project(1)
    steps(1)
    mod_arrived(1)
    project(2)
    steps(2)
    mod_last()
    prompt_send()
    project(3)
    wout_send()
    for index in range(8):
        attend_next(index)
        if index == 1:
            prompt_project()
        if index == 5:
            quarter_serve()
            prompt_attend()
        if index == 6:
            wout_serve()

    guide = guide_in[0]
    first_side = cfg == 0
    mix_out = []
    for h in range(heads):
        lanes = pl.ds(h * HEAD, HEAD)
        att_out[h].wait_recv()
        mine, other = att[h], peer[h]
        cond_part = jnp.where(first_side, mine, other)
        uncond = jnp.where(first_side, other, mine)
        mixed = (uncond + guide * (cond_part - uncond)).astype(BF16)
        mix[:, :, :, lanes] = mixed.reshape(4, 2, 64, HEAD)
        for d, half, group, part in (
            (2, 0, 3, 0), (2, 1, 3, 1), (1, 0, 2, 1), (1, 1, 1, 1), (3, 0, 1, 0), (3, 1, 2, 0),
        ):
            copy = remote(
                mix.at[group, part, :, lanes], mixall.at[seq, half, :, lanes],
                x_s.at[h, d - 1, half], x_r.at[h, seq, half], at_seq(d),
            )
            copy.start()
            mix_out.append(copy)
    total = jnp.dot(mix[0].reshape(128, width), wout[seq], preferred_element_type=F32)
    wout_last()
    for d in (1, 3, 2):
        c = (seq + d) % 4
        for h in range(heads):
            for half in range(2):
                here = mixall.at[c, half, :, pl.ds(h * HEAD, HEAD)]
                remote(here, here, x_s.at[0, 0, 0], x_r.at[h, c, half], at_seq(1)).wait_recv()
        total = total + jnp.dot(mixall[c].reshape(128, width), wout[c], preferred_element_type=F32)
    out_ref[...] = (table[2, pl.ds(now, 1), half_cols] * total).astype(BF16)

    for copy in sum(quarter_on, quarter_out) + mod_out[0] + mod_out[1] + prompt_out + pkv_out + wout_out + wout_pass + att_out + mix_out:
        copy.wait_send()
    for direction in range(2):
        mod_forward(direction).wait_send()
    each_stale(early, lambda copy: copy.wait_send())
    each_stale(late, lambda copy: copy.wait_send())
    for k in range(4):
        for condition, lane in ((pipe != 7, 0), (pipe != 0, 1), (pipe >= 0, 2)):
            pl.when(condition)(piece(sbuf.at[k], pipe, k, lane, at_x(1)).wait_send)
    for place in range(8):
        @pl.when(pipe == place)
        def _():
            for k in range(4):
                for whence in range(5):
                    for copy in passed(place, whence, k):
                        copy.wait_send()


def local(
    image_states, prompt_states, stale_kv, w_image_qkv, w_prompt_kv, w_output, mod_table, timestep, guidance
):
    rows, model = image_states.shape[1:]
    table = jnp.transpose(mod_table, (1, 0, 2))
    width = w_output.shape[0]
    heads = width // HEAD
    half = w_output.shape[1] // 2
    dma = pltpu.SemaphoreType.DMA
    anywhere = pl.BlockSpec(memory_space=pl.ANY)
    scalar = pl.BlockSpec(memory_space=pltpu.SMEM)
    return pl.pallas_call(
        kernel,
        out_shape=jax.ShapeDtypeStruct((rows, half), BF16),
        in_specs=[anywhere] * 7 + [scalar] * 2,
        out_specs=pl.BlockSpec(memory_space=pltpu.VMEM),
        scratch_shapes=[
            pltpu.VMEM((rows, model), BF16),
            pltpu.VMEM(table.shape, F32),
            pltpu.VMEM((16, model), BF16),
            pltpu.VMEM(w_image_qkv.shape, BF16),
            pltpu.VMEM(w_prompt_kv.shape, BF16),
            pltpu.VMEM((4, width, half), BF16),
            pltpu.VMEM((4, rows, model), BF16),
            pltpu.VMEM((4, 16, model), BF16),
            pltpu.VMEM((4, 2, 64, width), BF16),
            pltpu.VMEM((4, 2, rows, width), BF16),
            pltpu.VMEM((8, 4, 2, rows, width), BF16),
            pltpu.VMEM((heads, 4 * rows, HEAD), BF16),
            pltpu.VMEM((heads, 4 * rows, 2 * HEAD), F32),
            pltpu.VMEM((heads, 4 * rows, HEAD), F32),
            pltpu.VMEM((heads, 4 * rows, HEAD), F32),
            pltpu.VMEM((heads, 4 * rows, HEAD), F32),
            pltpu.VMEM((4, 2, rows // 2, width), BF16),
            pltpu.VMEM((4, 2, rows // 2, width), BF16),
            dma((10,)), dma((3, 4)), dma((4, 4)), dma((2, 2)), dma((2, 2)), dma((2,)), dma((2,)),
            dma((3,)), dma((4,)), dma((3,)), dma((4,)), dma((2,)), dma((2,)), dma((2,)), dma((2,)),
            dma((18, 4)), dma((8, 4)), dma((3,)), dma((4,)), dma((3, 3)), dma((4, 4)), dma((heads,)), dma((heads,)), dma((heads, 3, 2)), dma((heads, 4, 2)),
        ],
        compiler_params=pltpu.CompilerParams(
            collective_id=0, has_side_effects=True, vmem_limit_bytes=58 * 2**20
        ),
        name="guided_attention",
    )(image_states, prompt_states, stale_kv, w_image_qkv, w_prompt_kv, w_output, table, timestep, guidance)


def solution(mesh):
    return jax.shard_map(
        local,
        mesh=mesh,
        in_specs=(
            P("cfg", ("dp", "pipe", "seq"), None),
            P("cfg", ("dp", "seq"), None),
            P("cfg", None, ("dp", "pipe", "seq"), None),
            P(None, None, "seq"),
            P(None, None, "seq"),
            P("seq", None),
            P(),
            P("dp"),
            P("dp"),
        ),
        out_specs=P(("dp", "pipe", "seq"), "cfg"),
        check_vma=False,
    )
```

```python
import math

import jax
import jax.numpy as jnp
from jax import lax
from jax.experimental import pallas as pl
from jax.experimental.pallas import tpu as pltpu
from jax.sharding import PartitionSpec as P

MESH = pl.DeviceIdType.MESH
HEAD = 128
BF16 = jnp.bfloat16
F32 = jnp.float32


PLAN = (
    ((), (8, 19), (17, 18), (), (16,), (11, 12, 10, 1, 14, 9), (13,), (3,), (15,), (), ()),
    ((0, 20, 16), (1, 18, 4, 5), (14, 21, 2), (), (22, 23, 3, 17), (6,), (7, 19), (), (), (15,), ()),
    ((0, 4, 20, 16, 21), (18, 1, 12), (13, 15), (), (22, 2, 17, 23, 14), (3,), (6, 19), (), (), (), ()),
    ((20, 0, 16, 17), (8, 21, 1, 19, 18), (15, 13), (14,), (22, 2), (23, 12), (3,), (9,), (), (), ()),
    ((21, 16, 23, 22, 17), (20, 4, 6, 8, 18), (9, 5, 19), (), (), (12, 10, 7), (11,), (13,), (), (), ()),
    ((20, 0, 22, 5, 8, 6), (4, 16, 21), (9, 18), (), (23, 10), (17, 2, 19), (7,), (), (11,), (), ()),
    ((20, 21, 0, 22, 16, 4, 5), (7, 1), (6, 2, 23), (17, 18), (), (19, 3), (), (10,), (11,), (), ()),
    ((20, 21, 22, 23, 16), (8, 17, 13), (5, 9, 18), (12,), (14, 19), (15,), (), (10, 7), (), (11,), ()),
)
ATTEND = (
    (0, 4, 7, 1, 3, 5, 2, 6),
    (1, 0, 4, 2, 5, 7, 6, 3),
    (2, 7, 1, 6, 0, 3, 4, 5),
    (3, 7, 4, 2, 1, 0, 6, 5),
    (4, 0, 5, 3, 7, 1, 6, 2),
    (5, 7, 1, 6, 4, 0, 3, 2),
    (6, 7, 2, 5, 3, 1, 4, 0),
    (7, 3, 0, 6, 4, 5, 2, 1),
)
EARLY = (0, 2, 2, 2, 4, 3, 4, 4)

def passes_to(place, whence, k):
    upper, x = divmod(place, 4)
    if not upper:
        x = 3 - x
        whence = (1, 0, 3, 2, 4)[whence]
    far, near = k in (2, 3), k in (0, 1, 2, 3)
    ways = {
        0: "+" if x == 2 or (x == 1 and k % 2 == 0) or (x == 0 and not near) else "",
        1: ("-" if x == 1 or (x == 2 and near) or (x == 3 and k % 2 == 1) else "") + ("z" if x < 3 else ""),
        2: "+" if x != 2 or far else "",
        3: ("-" if x == 0 and not far else "") + ("z" if x == 3 else ""),
        4: "+-" if x == 3 else "-",
    }[whence]
    return ways if upper else ways.translate(str.maketrans("+-", "-+"))


def patch_from(place, whence):
    upper, x = divmod(place, 4)
    d = (3, 1, 3, 1, 0)[whence]
    return (upper if whence < 2 else 1 - upper) * 4 + (x + d) % 4


def awaited(place, patch, k):
    return any(patch_from(place, w) == patch and passes_to(place, w, k) for w in range(5))


def normalized(rows):
    center = rows - jnp.mean(rows, axis=-1, keepdims=True)
    spread = jnp.mean(center * center, axis=-1, keepdims=True)
    return center * lax.rsqrt(spread + 1e-06)


def kernel(
    img_in, prm_in, stale_in, wqkv_in, wpr_in, wout_in, table_in, step_in, guide_in,
    out_ref,
    img, table, prm, wqkv, wpr, wout, modbuf, prb, pkv, sbuf, kv, q, acc, top, att, peer, mix, mixall,
    lsem, st_s, st_r, m_s, m_r, mf_s, mf_r, pr_s, pr_r, pk_s, pk_r, w_s, w_r, wf_s, wf_r, ss, rs, v_s, v_r, u_s, u_r,
    a_s, a_r, x_s, x_r,
):
    dp, cfg, pipe, seq = (lax.axis_index(name) for name in ("dp", "cfg", "pipe", "seq"))
    x, zh = pipe % 4, pipe // 4
    heads, width = q.shape[0], kv.shape[-1]
    out_half = wout.shape[-1]
    model = img.shape[-1]
    scale = math.log2(math.e) / math.sqrt(HEAD)

    def at_seq(d):
        return (dp, cfg, pipe, (seq + d) % 4)

    def at_x(d):
        return (dp, cfg, zh * 4 + (x + d) % 4, seq)

    at_z = (dp, cfg, (1 - zh) * 4 + x, seq)
    at_core = (dp, 1 - cfg, pipe, seq)
    line = zh * 2 + dp
    at_line = [(1 - dp, cfg, pipe, seq), at_z, (1 - dp, cfg, (1 - zh) * 4 + x, seq)]
    line_of = [zh * 2 + 1 - dp, (1 - zh) * 2 + dp, (1 - zh) * 2 + 1 - dp]

    def remote(src, dst, s, r, device):
        return pltpu.make_async_remote_copy(
            src_ref=src, dst_ref=dst, send_sem=s, recv_sem=r, device_id=device, device_id_type=MESH
        )

    barrier = pltpu.get_barrier_semaphore()
    partners = [at_seq(1), at_seq(3), at_seq(2), at_x(1), at_x(3), at_x(2), at_core] + at_line
    for device in partners:
        pl.semaphore_signal(barrier, inc=1, device_id=device, device_id_type=MESH)

    half_cols = pl.ds(pl.multiple_of(cfg * out_half, 128), out_half)

    def seq_cols(d):
        return pl.ds(pl.multiple_of((seq + d) % 4 * width, 128), width)

    def stale_part(k, source):
        return sbuf.at[k, :, pl.ds(pl.multiple_of(source * 32, 32), 32)]

    loads = [
        pltpu.make_async_copy(img_in.at[0], img, lsem.at[0]),
        pltpu.make_async_copy(table_in, table, lsem.at[1]),
        pltpu.make_async_copy(prm_in.at[0, pl.ds(pl.multiple_of(x * 16, 16), 16)], prm, lsem.at[2]),
        pltpu.make_async_copy(wqkv_in, wqkv, lsem.at[3]),
        pltpu.make_async_copy(stale_in.at[0, :, pl.ds(0, 32), seq_cols(0)], stale_part(0, seq), lsem.at[4]),
        pltpu.make_async_copy(wpr_in, wpr, lsem.at[5]),
        pltpu.make_async_copy(wout_in.at[:, half_cols], wout.at[seq], lsem.at[6]),
    ] + [
        pltpu.make_async_copy(
            stale_in.at[0, :, pl.ds(k * 32, 32), seq_cols(0)], stale_part(k, seq), lsem.at[6 + k]
        )
        for k in (1, 2, 3)
    ]
    for load in loads:
        load.start()

    now = step_in[0]
    loads[0].wait()
    loads[1].wait()

    def modulate(first, count):
        def rows16(i, carry):
            rows = pl.ds(pl.multiple_of(first + i * 16, 16), 16)
            shift, gain = table[0, pl.ds(now, 1), :], table[1, pl.ds(now, 1), :]
            values = normalized(img[rows, :].astype(F32)) * (1.0 + gain) + shift
            modbuf[0, rows, :] = values.astype(BF16)
            return carry

        lax.fori_loop(0, count // 16, rows16, 0)

    modulate(0, 64)
    pl.semaphore_wait(barrier, len(partners))

    def any_of(places):
        found = pipe == places[0]
        for place in places[1:]:
            found = found | (pipe == place)
        return found

    def stale_copy(k, d, source):
        return remote(
            stale_in.at[0, :, pl.ds(k * 32, 32), seq_cols(d)], stale_part(k, source),
            st_s.at[d - 1, k], st_r.at[source, k], at_seq(d),
        )

    stale_out = [[stale_copy(k, d, seq) for d in (2, 1, 3)] for k in range(4)]
    early = [[place for place in range(1, 8) if EARLY[place] > k] for k in range(4)]
    late = [[place for place in range(1, 8) if EARLY[place] <= k] for k in range(4)]

    def each_stale(places, act):
        for k in range(4):
            if places[k]:
                @pl.when(any_of(places[k]))
                def _():
                    for copy in stale_out[k]:
                        act(copy)

    each_stale(early, lambda copy: copy.start())
    modulate(64, 64)

    def half_rows(half):
        return pl.ds(half * 64, 64)

    def mod_copy(direction, order):
        half = direction if order == 0 else 1 - direction
        source = modbuf.at[0, half_rows(half)]
        target = modbuf.at[1 + order, half_rows(direction)]
        return remote(
            source, target, m_s.at[direction, order], m_r.at[direction, order], at_seq(1 if direction == 0 else 3)
        )

    def mod_forward(direction):
        source = modbuf.at[1, half_rows(direction)]
        target = modbuf.at[3, half_rows(direction)]
        return remote(source, target, mf_s.at[direction], mf_r.at[direction], at_seq(1 if direction == 0 else 3))

    mod_out = [[mod_copy(a, b) for b in range(2)] for a in range(2)]

    def piece(source, slot, k, lane, device):
        return remote(source, kv.at[slot, k], ss.at[lane, k], rs.at[slot, k], device)

    att_out = [remote(att.at[h], peer.at[h], a_s.at[h], a_r.at[h], at_core) for h in range(heads)]

    def send_attended(h):
        block = acc[h]
        att[h] = block[:, :HEAD] / block[:, HEAD : HEAD + 1]
        att_out[h].start()

    def toward(way):
        return {"+": at_x(1), "-": at_x(3), "z": at_z}[way]

    def send_own(k):
        for condition, lane, way in ((x < 3, 0, "+"), (pipe == 4, 1, "-"), (zh == 0, 2, "z")):
            pl.when(condition)(piece(kv.at[pipe, k], pipe, k, lane, toward(way)).start)

    def send_stale(place, k):
        upper, column = divmod(place, 4)
        for d in (1, 3, 2):
            stale_copy(k, d, (seq + d) % 4).wait_recv()
        ways = (("+", 0),) * (place == 3) + (("-", 1),) * (column > 0) + (("z", 2),) * upper
        for way, lane in ways:
            piece(sbuf.at[k], place, k, lane, toward(way)).start()

    def landed(slot, k):
        here = kv.at[slot, k]
        remote(here, here, ss.at[0, 0], rs.at[slot, k], at_x(1)).wait_recv()

    def passed(place, whence, k):
        slot = patch_from(place, whence)
        for way in passes_to(place, whence, k):
            yield piece(kv.at[slot, k], slot, k, 3 + 3 * whence + "+-z".index(way), toward(way))

    def step(place, code):
        whence, k = divmod(code, 4)
        if whence == 5:
            send_stale(place, k)
            return
        landed(patch_from(place, whence), k)
        for copy in passed(place, whence, k):
            copy.start()

    def steps(index):
        for place in range(8):
            if PLAN[place][index]:
                @pl.when(pipe == place)
                def _():
                    for code in PLAN[place][index]:
                        step(place, code)

    def attend_next(index):
        steps(3 + index)
        slot = 0
        for place in range(8):
            patch = ATTEND[place][index]
            slot = slot + jnp.where(pipe == place, patch, 0)
            rest = [k for k in range(4) if patch != place and not awaited(place, patch, k)]
            if rest:
                @pl.when(pipe == place)
                def _():
                    for k in rest:
                        landed(patch, k)
        attend_slot(slot, index == 0, send_attended if index == 7 else None)

    def project(k):
        rows = modbuf[k]
        for j in (1, 2):
            kv[pipe, k, j - 1] = jnp.dot(rows, wqkv[j], preferred_element_type=F32).astype(BF16)
        send_own(k)
        block = jnp.dot(rows, wqkv[0], preferred_element_type=F32).astype(BF16)
        for h in range(heads):
            q[h, k * 128 : (k + 1) * 128, :] = block[:, h * HEAD : (h + 1) * HEAD]

    def late_in(k):
        when(x > 0, serve, 0, k)
        when(x == 3, serve, 1, k)

    def late_far(k):
        when(upper, serve, 4, k)

    def late_far_two(k):
        when(upper, serve, 2, k)
        when(upper, serve, 3, k)

    def early_in(k):
        when(x == 0, serve, 0, k)
        when(x < 3, serve, 1, k)

    def early_far(k):
        when(zh == 0, serve, 4, k)

    def early_far_two(k):
        when(zh == 0, serve, 2, k)
        when(zh == 0, serve, 3, k)

    def mod_arrived(order):
        for direction in range(2):
            mod_out[direction][order].wait_recv()
            if order == 0:
                mod_forward(direction).start()

    def attend_head(h, keys, values, first):
        values = jnp.concatenate([values, jnp.ones_like(values)], axis=1)
        scores = lax.dot_general(q[h], keys, (((1,), (1,)), ((), ())), preferred_element_type=F32)
        peak = jnp.max(scores, axis=1, keepdims=True)
        if first:
            new_top = peak
        else:
            old_top = top[h][:, :1]
            new_top = jnp.maximum(old_top, peak)
        weights = jnp.exp2(scores * scale - new_top * scale).astype(BF16)
        part = jnp.dot(weights, values, preferred_element_type=F32)
        if first:
            acc[h] = part
        else:
            acc[h] = acc[h] * jnp.exp2((old_top - new_top) * scale) + part
        top[h] = jnp.broadcast_to(new_top, top.shape[1:])

    def attend(keys_of, values_of, first, finish=None):
        for h in range(heads):
            lanes = pl.ds(h * HEAD, HEAD)
            attend_head(h, keys_of(lanes), values_of(lanes), first)
            if finish is not None:
                finish(h)


    def attend_slot(slot, first=False, finish=None):
        attend(
            lambda lanes: kv[slot, :, 0, :, lanes].reshape(512, HEAD),
            lambda lanes: kv[slot, :, 1, :, lanes].reshape(512, HEAD),
            first,
            finish,
        )

    def start_mod():
        for order in range(2):
            for direction in range(2):
                mod_out[direction][order].start()

    prompt_out = [
        remote(prb.at[seq], prb.at[seq], pr_s.at[d - 1], pr_r.at[seq], at_seq(d)) for d in (1, 3, 2)
    ]
    pkv_out = [remote(pkv.at[x], pkv.at[x], pk_s.at[d - 1], pk_r.at[x], at_x(d)) for d in (1, 3, 2)]

    def prompt_rows():
        loads[2].wait()
        prb[seq] = normalized(prm[...].astype(F32)).astype(BF16)

    def prompt_send():
        for copy in prompt_out:
            copy.start()

    def prompt_project():
        loads[5].wait()
        for d in (1, 3, 2):
            c = (seq + d) % 4
            remote(prb.at[c], prb.at[c], pr_s.at[0], pr_r.at[c], at_seq(1)).wait_recv()
        rows = prb[...].reshape(64, model)
        for j in range(2):
            pkv[x, j] = jnp.dot(rows, wpr[j], preferred_element_type=F32).astype(BF16)
        for copy in pkv_out:
            copy.start()

    def prompt_attend():
        for d in (1, 3, 2):
            c = (x + d) % 4
            remote(pkv.at[c], pkv.at[c], pk_s.at[0], pk_r.at[c], at_x(1)).wait_recv()
        attend(
            lambda lanes: pkv[:, 0, :, lanes].reshape(256, HEAD),
            lambda lanes: pkv[:, 1, :, lanes].reshape(256, HEAD),
            False,
        )

    share = out_half // 3
    quarter = width // 4

    def wout_copy(direction):
        part = wout.at[seq, :, pl.ds(0, out_half - share)]
        return remote(part, part, w_s.at[direction], w_r.at[direction], at_seq(1 if direction == 0 else 3))

    def wout_arrival(direction):
        part = wout.at[(seq + (3 if direction == 0 else 1)) % 4, :, pl.ds(0, out_half - share)]
        return remote(part, part, w_s.at[direction], w_r.at[direction], at_seq(1))

    def wout_forward(direction, source):
        part = wout.at[source, pl.ds(direction * (width // 2), width // 2), pl.ds(0, out_half - share)]
        return remote(part, part, wf_s.at[direction], wf_r.at[direction], at_seq(1 if direction == 0 else 3))

    def wout_quarter(source, place):
        rows = pl.ds(pl.multiple_of(place * quarter, 16), quarter)
        return wout.at[source, rows, pl.ds(out_half - share, share)]

    def quarter_copy(source, d):
        part = wout_quarter(source, line)
        return remote(part, part, v_s.at[d - 1], v_r.at[source], at_seq(d))

    def quarter_pass(d, to):
        source = (seq + d) % 4
        part = wout_quarter(source, line)
        return remote(part, part, u_s.at[d - 1, to], u_r.at[source, line], at_line[to])

    def quarter_arrival(d, place):
        source = (seq + d) % 4
        part = wout_quarter(source, place)
        return remote(part, part, u_s.at[0, 0], u_r.at[source, place], at_line[0])

    wout_out = [wout_copy(direction) for direction in range(2)]
    wout_pass = [wout_forward(direction, (seq + (3 if direction == 0 else 1)) % 4) for direction in range(2)]
    quarter_out = [quarter_copy(seq, d) for d in (2, 1, 3)]
    quarter_on = [[quarter_pass(d, to) for to in range(3)] for d in (1, 3, 2)]

    def wout_send():
        loads[6].wait()
        for copy in quarter_out + wout_out:
            copy.start()

    def quarter_serve():
        for d, copies in zip((1, 3, 2), quarter_on):
            quarter_copy((seq + d) % 4, 1).wait_recv()
            for copy in copies:
                copy.start()

    def wout_serve():
        for direction in range(2):
            wout_arrival(direction).wait_recv()
            wout_pass[direction].start()

    def wout_last():
        for direction in range(2):
            wout_forward(direction, (seq + 2) % 4).wait_recv()
        for d in (1, 3, 2):
            for place in line_of:
                quarter_arrival(d, place).wait_recv()

    def mod_last():
        for direction in range(2):
            mod_forward(direction).wait_recv()

    start_mod()
    loads[3].wait()
    project(0)
    for load in [loads[4]] + loads[7:]:
        load.wait()
    prompt_rows()
    steps(0)
    mod_arrived(0)
    each_stale(late, lambda copy: copy.start())
    project(1)
    steps(1)
    mod_arrived(1)
    project(2)
    steps(2)
    mod_last()
    prompt_send()
    project(3)
    wout_send()
    for index in range(8):
        attend_next(index)
        if index == 1:
            prompt_project()
        if index == 5:
            quarter_serve()
            prompt_attend()
        if index == 6:
            wout_serve()

    guide = guide_in[0]
    first_side = cfg == 0
    mix_out = []
    for h in range(heads):
        lanes = pl.ds(h * HEAD, HEAD)
        att_out[h].wait_recv()
        mine, other = att[h], peer[h]
        cond_part = jnp.where(first_side, mine, other)
        uncond = jnp.where(first_side, other, mine)
        mixed = (uncond + guide * (cond_part - uncond)).astype(BF16)
        mix[:, :, :, lanes] = mixed.reshape(4, 2, 64, HEAD)
        for d, half, group, part in (
            (2, 0, 3, 0), (2, 1, 3, 1), (1, 0, 2, 1), (1, 1, 1, 1), (3, 0, 1, 0), (3, 1, 2, 0),
        ):
            copy = remote(
                mix.at[group, part, :, lanes], mixall.at[seq, half, :, lanes],
                x_s.at[h, d - 1, half], x_r.at[h, seq, half], at_seq(d),
            )
            copy.start()
            mix_out.append(copy)
    total = jnp.dot(mix[0].reshape(128, width), wout[seq], preferred_element_type=F32)
    wout_last()
    for d in (1, 3, 2):
        c = (seq + d) % 4
        for h in range(heads):
            for half in range(2):
                here = mixall.at[c, half, :, pl.ds(h * HEAD, HEAD)]
                remote(here, here, x_s.at[0, 0, 0], x_r.at[h, c, half], at_seq(1)).wait_recv()
        total = total + jnp.dot(mixall[c].reshape(128, width), wout[c], preferred_element_type=F32)
    out_ref[...] = (table[2, pl.ds(now, 1), half_cols] * total).astype(BF16)

    for copy in sum(quarter_on, quarter_out) + mod_out[0] + mod_out[1] + prompt_out + pkv_out + wout_out + wout_pass + att_out + mix_out:
        copy.wait_send()
    for direction in range(2):
        mod_forward(direction).wait_send()
    each_stale(early, lambda copy: copy.wait_send())
    each_stale(late, lambda copy: copy.wait_send())
    for k in range(4):
        for condition, lane in ((pipe != 7, 0), (pipe != 0, 1), (pipe >= 0, 2)):
            pl.when(condition)(piece(sbuf.at[k], pipe, k, lane, at_x(1)).wait_send)
    for place in range(8):
        @pl.when(pipe == place)
        def _():
            for k in range(4):
                for whence in range(5):
                    for copy in passed(place, whence, k):
                        copy.wait_send()


def local(
    image_states, prompt_states, stale_kv, w_image_qkv, w_prompt_kv, w_output, mod_table, timestep, guidance
):
    rows, model = image_states.shape[1:]
    table = jnp.transpose(mod_table, (1, 0, 2))
    width = w_output.shape[0]
    heads = width // HEAD
    half = w_output.shape[1] // 2
    dma = pltpu.SemaphoreType.DMA
    anywhere = pl.BlockSpec(memory_space=pl.ANY)
    scalar = pl.BlockSpec(memory_space=pltpu.SMEM)
    return pl.pallas_call(
        kernel,
        out_shape=jax.ShapeDtypeStruct((rows, half), BF16),
        in_specs=[anywhere] * 7 + [scalar] * 2,
        out_specs=pl.BlockSpec(memory_space=pltpu.VMEM),
        scratch_shapes=[
            pltpu.VMEM((rows, model), BF16),
            pltpu.VMEM(table.shape, F32),
            pltpu.VMEM((16, model), BF16),
            pltpu.VMEM(w_image_qkv.shape, BF16),
            pltpu.VMEM(w_prompt_kv.shape, BF16),
            pltpu.VMEM((4, width, half), BF16),
            pltpu.VMEM((4, rows, model), BF16),
            pltpu.VMEM((4, 16, model), BF16),
            pltpu.VMEM((4, 2, 64, width), BF16),
            pltpu.VMEM((4, 2, rows, width), BF16),
            pltpu.VMEM((8, 4, 2, rows, width), BF16),
            pltpu.VMEM((heads, 4 * rows, HEAD), BF16),
            pltpu.VMEM((heads, 4 * rows, 2 * HEAD), F32),
            pltpu.VMEM((heads, 4 * rows, HEAD), F32),
            pltpu.VMEM((heads, 4 * rows, HEAD), F32),
            pltpu.VMEM((heads, 4 * rows, HEAD), F32),
            pltpu.VMEM((4, 2, rows // 2, width), BF16),
            pltpu.VMEM((4, 2, rows // 2, width), BF16),
            dma((10,)), dma((3, 4)), dma((4, 4)), dma((2, 2)), dma((2, 2)), dma((2,)), dma((2,)),
            dma((3,)), dma((4,)), dma((3,)), dma((4,)), dma((2,)), dma((2,)), dma((2,)), dma((2,)),
            dma((18, 4)), dma((8, 4)), dma((3,)), dma((4,)), dma((3, 3)), dma((4, 4)), dma((heads,)), dma((heads,)), dma((heads, 3, 2)), dma((heads, 4, 2)),
        ],
        compiler_params=pltpu.CompilerParams(
            collective_id=0, has_side_effects=True, vmem_limit_bytes=58 * 2**20
        ),
        name="guided_attention",
    )(image_states, prompt_states, stale_kv, w_image_qkv, w_prompt_kv, w_output, table, timestep, guidance)


def solution(mesh):
    return jax.shard_map(
        local,
        mesh=mesh,
        in_specs=(
            P("cfg", ("dp", "pipe", "seq"), None),
            P("cfg", ("dp", "seq"), None),
            P("cfg", None, ("dp", "pipe", "seq"), None),
            P(None, None, "seq"),
            P(None, None, "seq"),
            P("seq", None),
            P(),
            P("dp"),
            P("dp"),
        ),
        out_specs=P(("dp", "pipe", "seq"), "cfg"),
        check_vma=False,
    )
```

```python
import math

import jax
import jax.numpy as jnp
from jax import lax
from jax.experimental import pallas as pl
from jax.experimental.pallas import tpu as pltpu
from jax.sharding import PartitionSpec as P

MESH = pl.DeviceIdType.MESH
HEAD = 128
BF16 = jnp.bfloat16
F32 = jnp.float32


PLAN = (
    ((), (17, 1, 18), (9, 16), (12, 19), (), (8, 14, 10, 13, 11), (3,), (), (), (15,), ()),
    ((20, 0, 4, 16, 5, 17), (1, 18, 21), (15, 14), (), (22, 2, 23, 3), (6, 19), (), (7,), (), (), ()),
    ((20, 21, 0, 17, 4), (12, 6, 19), (1, 13), (15,), (22, 16, 2, 23, 18, 14, 3), (), (), (), (), (), ()),
    ((21, 20, 22, 0, 17), (13, 9, 1, 16, 18), (19, 2, 14), (), (23, 12), (3, 15), (), (8,), (), (), ()),
    ((21, 22, 4, 16, 20, 23, 17), (6, 5), (18, 9, 19), (8, 12), (), (10, 7), (13,), (11,), (), (), ()),
    ((20, 21, 22, 0, 5), (8, 7, 6, 16), (9, 18), (), (23, 17, 4), (2, 19), (), (10,), (11,), (), ()),
    ((21, 0, 4, 23, 22, 16, 5), (7, 20, 17, 1), (6, 18, 2), (), (), (19, 3), (), (10, 11), (), (), ()),
    ((20, 21, 22, 23, 12, 8), (16, 13, 17), (9, 18), (), (10, 14, 5, 19, 15), (), (), (11, 7), (), (), ()),
)
ATTEND = (
    (0, 4, 7, 3, 1, 6, 5, 2),
    (1, 0, 5, 4, 2, 6, 3, 7),
    (2, 6, 7, 1, 3, 0, 4, 5),
    (3, 7, 2, 4, 6, 0, 1, 5),
    (4, 0, 5, 7, 3, 6, 2, 1),
    (5, 6, 1, 4, 7, 0, 2, 3),
    (6, 7, 2, 5, 1, 3, 4, 0),
    (7, 3, 6, 0, 5, 2, 4, 1),
)
EARLY = (0, 2, 2, 3, 4, 3, 4, 4)

def passes_to(place, whence, k):
    upper, x = divmod(place, 4)
    if not upper:
        x = 3 - x
        whence = (1, 0, 3, 2, 4)[whence]
    far, near = k in (2, 3), k in (0, 1, 2, 3)
    ways = {
        0: "+" if x == 2 or (x == 1 and k % 2 == 0) or (x == 0 and not near) else "",
        1: ("-" if x == 1 or (x == 2 and near) or (x == 3 and k % 2 == 1) else "") + ("z" if x < 3 else ""),
        2: "+" if x != 2 or far else "",
        3: ("-" if x == 0 and not far else "") + ("z" if x == 3 else ""),
        4: "+-" if x == 3 else "-",
    }[whence]
    return ways if upper else ways.translate(str.maketrans("+-", "-+"))


def patch_from(place, whence):
    upper, x = divmod(place, 4)
    d = (3, 1, 3, 1, 0)[whence]
    return (upper if whence < 2 else 1 - upper) * 4 + (x + d) % 4


def awaited(place, patch, k):
    return any(patch_from(place, w) == patch and passes_to(place, w, k) for w in range(5))


def normalized(rows):
    center = rows - jnp.mean(rows, axis=-1, keepdims=True)
    spread = jnp.mean(center * center, axis=-1, keepdims=True)
    return center * lax.rsqrt(spread + 1e-06)


def kernel(
    img_in, prm_in, stale_in, wqkv_in, wpr_in, wout_in, table_in, step_in, guide_in,
    out_ref,
    img, table, prm, wqkv, wpr, wout, modbuf, prb, pkv, sbuf, kv, q, acc, top, att, peer, mix, mixall,
    lsem, st_s, st_r, m_s, m_r, mf_s, mf_r, pr_s, pr_r, pk_s, pk_r, w_s, w_r, wf_s, wf_r, ss, rs, v_s, v_r, u_s, u_r,
    a_s, a_r, x_s, x_r,
):
    dp, cfg, pipe, seq = (lax.axis_index(name) for name in ("dp", "cfg", "pipe", "seq"))
    x, zh = pipe % 4, pipe // 4
    heads, width = q.shape[0], kv.shape[-1]
    out_half = wout.shape[-1]
    model = img.shape[-1]
    scale = math.log2(math.e) / math.sqrt(HEAD)

    def at_seq(d):
        return (dp, cfg, pipe, (seq + d) % 4)

    def at_x(d):
        return (dp, cfg, zh * 4 + (x + d) % 4, seq)

    at_z = (dp, cfg, (1 - zh) * 4 + x, seq)
    at_core = (dp, 1 - cfg, pipe, seq)
    line = zh * 2 + dp
    at_line = [(1 - dp, cfg, pipe, seq), at_z, (1 - dp, cfg, (1 - zh) * 4 + x, seq)]
    line_of = [zh * 2 + 1 - dp, (1 - zh) * 2 + dp, (1 - zh) * 2 + 1 - dp]

    def remote(src, dst, s, r, device):
        return pltpu.make_async_remote_copy(
            src_ref=src, dst_ref=dst, send_sem=s, recv_sem=r, device_id=device, device_id_type=MESH
        )

    barrier = pltpu.get_barrier_semaphore()
    partners = [at_seq(1), at_seq(3), at_seq(2), at_x(1), at_x(3), at_x(2), at_core] + at_line
    for device in partners:
        pl.semaphore_signal(barrier, inc=1, device_id=device, device_id_type=MESH)

    half_cols = pl.ds(pl.multiple_of(cfg * out_half, 128), out_half)

    def seq_cols(d):
        return pl.ds(pl.multiple_of((seq + d) % 4 * width, 128), width)

    def stale_part(k, source):
        return sbuf.at[k, :, pl.ds(pl.multiple_of(source * 32, 32), 32)]

    loads = [
        pltpu.make_async_copy(img_in.at[0], img, lsem.at[0]),
        pltpu.make_async_copy(table_in, table, lsem.at[1]),
        pltpu.make_async_copy(prm_in.at[0, pl.ds(pl.multiple_of(x * 16, 16), 16)], prm, lsem.at[2]),
        pltpu.make_async_copy(wqkv_in, wqkv, lsem.at[3]),
        pltpu.make_async_copy(stale_in.at[0, :, pl.ds(0, 32), seq_cols(0)], stale_part(0, seq), lsem.at[4]),
        pltpu.make_async_copy(wpr_in, wpr, lsem.at[5]),
        pltpu.make_async_copy(wout_in.at[:, half_cols], wout.at[seq], lsem.at[6]),
    ] + [
        pltpu.make_async_copy(
            stale_in.at[0, :, pl.ds(k * 32, 32), seq_cols(0)], stale_part(k, seq), lsem.at[6 + k]
        )
        for k in (1, 2, 3)
    ]
    for load in loads:
        load.start()

    now = step_in[0]
    loads[0].wait()
    loads[1].wait()

    def modulate(first, count):
        def rows16(i, carry):
            rows = pl.ds(pl.multiple_of(first + i * 16, 16), 16)
            shift, gain = table[0, pl.ds(now, 1), :], table[1, pl.ds(now, 1), :]
            values = normalized(img[rows, :].astype(F32)) * (1.0 + gain) + shift
            modbuf[0, rows, :] = values.astype(BF16)
            return carry

        lax.fori_loop(0, count // 16, rows16, 0)

    modulate(0, 64)
    pl.semaphore_wait(barrier, len(partners))

    def any_of(places):
        found = pipe == places[0]
        for place in places[1:]:
            found = found | (pipe == place)
        return found

    def stale_copy(k, d, source):
        return remote(
            stale_in.at[0, :, pl.ds(k * 32, 32), seq_cols(d)], stale_part(k, source),
            st_s.at[d - 1, k], st_r.at[source, k], at_seq(d),
        )

    stale_out = [[stale_copy(k, d, seq) for d in (2, 1, 3)] for k in range(4)]
    early = [[place for place in range(1, 8) if EARLY[place] > k] for k in range(4)]
    late = [[place for place in range(1, 8) if EARLY[place] <= k] for k in range(4)]

    def each_stale(places, act):
        for k in range(4):
            if places[k]:
                @pl.when(any_of(places[k]))
                def _():
                    for copy in stale_out[k]:
                        act(copy)

    each_stale(early, lambda copy: copy.start())
    modulate(64, 64)

    def half_rows(half):
        return pl.ds(half * 64, 64)

    def mod_copy(direction, order):
        half = direction if order == 0 else 1 - direction
        source = modbuf.at[0, half_rows(half)]
        target = modbuf.at[1 + order, half_rows(direction)]
        return remote(
            source, target, m_s.at[direction, order], m_r.at[direction, order], at_seq(1 if direction == 0 else 3)
        )

    def mod_forward(direction):
        source = modbuf.at[1, half_rows(direction)]
        target = modbuf.at[3, half_rows(direction)]
        return remote(source, target, mf_s.at[direction], mf_r.at[direction], at_seq(1 if direction == 0 else 3))

    mod_out = [[mod_copy(a, b) for b in range(2)] for a in range(2)]

    def piece(source, slot, k, lane, device):
        return remote(source, kv.at[slot, k], ss.at[lane, k], rs.at[slot, k], device)

    att_out = [remote(att.at[h], peer.at[h], a_s.at[h], a_r.at[h], at_core) for h in range(heads)]

    def send_attended(h):
        block = acc[h]
        att[h] = block[:, :HEAD] / block[:, HEAD : HEAD + 1]
        att_out[h].start()

    def toward(way):
        return {"+": at_x(1), "-": at_x(3), "z": at_z}[way]

    def send_own(k):
        for condition, lane, way in ((x < 3, 0, "+"), (pipe == 4, 1, "-"), (zh == 0, 2, "z")):
            pl.when(condition)(piece(kv.at[pipe, k], pipe, k, lane, toward(way)).start)

    def send_stale(place, k):
        upper, column = divmod(place, 4)
        for d in (1, 3, 2):
            stale_copy(k, d, (seq + d) % 4).wait_recv()
        ways = (("+", 0),) * (place == 3) + (("-", 1),) * (column > 0) + (("z", 2),) * upper
        for way, lane in ways:
            piece(sbuf.at[k], place, k, lane, toward(way)).start()

    def landed(slot, k):
        here = kv.at[slot, k]
        remote(here, here, ss.at[0, 0], rs.at[slot, k], at_x(1)).wait_recv()

    def passed(place, whence, k):
        slot = patch_from(place, whence)
        for way in passes_to(place, whence, k):
            yield piece(kv.at[slot, k], slot, k, 3 + 3 * whence + "+-z".index(way), toward(way))

    def step(place, code):
        whence, k = divmod(code, 4)
        if whence == 5:
            send_stale(place, k)
            return
        landed(patch_from(place, whence), k)
        for copy in passed(place, whence, k):
            copy.start()

    def steps(index):
        for place in range(8):
            if PLAN[place][index]:
                @pl.when(pipe == place)
                def _():
                    for code in PLAN[place][index]:
                        step(place, code)

    def attend_next(index):
        steps(3 + index)
        slot = 0
        for place in range(8):
            patch = ATTEND[place][index]
            slot = slot + jnp.where(pipe == place, patch, 0)
            rest = [k for k in range(4) if patch != place and not awaited(place, patch, k)]
            if rest:
                @pl.when(pipe == place)
                def _():
                    for k in rest:
                        landed(patch, k)
        attend_slot(slot, index == 0, send_attended if index == 7 else None)

    def project(k):
        rows = modbuf[k]
        for j in (1, 2):
            kv[pipe, k, j - 1] = jnp.dot(rows, wqkv[j], preferred_element_type=F32).astype(BF16)
        send_own(k)
        block = jnp.dot(rows, wqkv[0], preferred_element_type=F32).astype(BF16)
        for h in range(heads):
            q[h, k * 128 : (k + 1) * 128, :] = block[:, h * HEAD : (h + 1) * HEAD]

    def late_in(k):
        when(x > 0, serve, 0, k)
        when(x == 3, serve, 1, k)

    def late_far(k):
        when(upper, serve, 4, k)

    def late_far_two(k):
        when(upper, serve, 2, k)
        when(upper, serve, 3, k)

    def early_in(k):
        when(x == 0, serve, 0, k)
        when(x < 3, serve, 1, k)

    def early_far(k):
        when(zh == 0, serve, 4, k)

    def early_far_two(k):
        when(zh == 0, serve, 2, k)
        when(zh == 0, serve, 3, k)

    def mod_arrived(order):
        for direction in range(2):
            mod_out[direction][order].wait_recv()
            if order == 0:
                mod_forward(direction).start()

    def attend_head(h, keys, values, first):
        values = jnp.concatenate([values, jnp.ones_like(values)], axis=1)
        scores = lax.dot_general(q[h], keys, (((1,), (1,)), ((), ())), preferred_element_type=F32)
        peak = jnp.max(scores, axis=1, keepdims=True)
        if first:
            new_top = peak
        else:
            old_top = top[h][:, :1]
            new_top = jnp.maximum(old_top, peak)
        weights = jnp.exp2(scores * scale - new_top * scale).astype(BF16)
        part = jnp.dot(weights, values, preferred_element_type=F32)
        if first:
            acc[h] = part
        else:
            acc[h] = acc[h] * jnp.exp2((old_top - new_top) * scale) + part
        top[h] = jnp.broadcast_to(new_top, top.shape[1:])

    def attend(keys_of, values_of, first, finish=None):
        for h in range(heads):
            lanes = pl.ds(h * HEAD, HEAD)
            attend_head(h, keys_of(lanes), values_of(lanes), first)
            if finish is not None:
                finish(h)


    def attend_slot(slot, first=False, finish=None):
        attend(
            lambda lanes: kv[slot, :, 0, :, lanes].reshape(512, HEAD),
            lambda lanes: kv[slot, :, 1, :, lanes].reshape(512, HEAD),
            first,
            finish,
        )

    def start_mod():
        for order in range(2):
            for direction in range(2):
                mod_out[direction][order].start()

    prompt_out = [
        remote(prb.at[seq], prb.at[seq], pr_s.at[d - 1], pr_r.at[seq], at_seq(d)) for d in (1, 3, 2)
    ]
    pkv_up = remote(pkv.at[x], pkv.at[x], pk_s.at[3], pk_r.at[x], at_z)
    pkv_out = [remote(pkv.at[x], pkv.at[x], pk_s.at[d - 1], pk_r.at[x], at_x(d)) for d in (1, 3, 2)]

    lower, upper = zh == 0, zh == 1

    def prompt_rows():
        loads[2].wait()

        @pl.when(lower)
        def _():
            prb[seq] = normalized(prm[...].astype(F32)).astype(BF16)

    def prompt_send():
        @pl.when(lower)
        def _():
            for copy in prompt_out:
                copy.start()

    def prompt_project():
        loads[5].wait()

        @pl.when(lower)
        def _():
            for d in (1, 3, 2):
                c = (seq + d) % 4
                remote(prb.at[c], prb.at[c], pr_s.at[0], pr_r.at[c], at_seq(1)).wait_recv()
            rows = prb[...].reshape(64, model)
            for j in range(2):
                pkv[x, j] = jnp.dot(rows, wpr[j], preferred_element_type=F32).astype(BF16)
            for copy in [pkv_up] + pkv_out:
                copy.start()

    def prompt_pass():
        @pl.when(upper)
        def _():
            pkv_up.wait_recv()
            for copy in pkv_out:
                copy.start()

    def prompt_attend():
        for d in (1, 3, 2):
            c = (x + d) % 4
            remote(pkv.at[c], pkv.at[c], pk_s.at[0], pk_r.at[c], at_x(1)).wait_recv()
        attend(
            lambda lanes: pkv[:, 0, :, lanes].reshape(256, HEAD),
            lambda lanes: pkv[:, 1, :, lanes].reshape(256, HEAD),
            False,
        )

    share = out_half // 3
    quarter = width // 4

    def wout_copy(direction):
        part = wout.at[seq, :, pl.ds(0, out_half - share)]
        return remote(part, part, w_s.at[direction], w_r.at[direction], at_seq(1 if direction == 0 else 3))

    def wout_arrival(direction):
        part = wout.at[(seq + (3 if direction == 0 else 1)) % 4, :, pl.ds(0, out_half - share)]
        return remote(part, part, w_s.at[direction], w_r.at[direction], at_seq(1))

    def wout_forward(direction, source):
        part = wout.at[source, pl.ds(direction * (width // 2), width // 2), pl.ds(0, out_half - share)]
        return remote(part, part, wf_s.at[direction], wf_r.at[direction], at_seq(1 if direction == 0 else 3))

    def wout_quarter(source, place):
        rows = pl.ds(pl.multiple_of(place * quarter, 16), quarter)
        return wout.at[source, rows, pl.ds(out_half - share, share)]

    def quarter_copy(source, d):
        part = wout_quarter(source, line)
        return remote(part, part, v_s.at[d - 1], v_r.at[source], at_seq(d))

    def quarter_pass(d, to):
        source = (seq + d) % 4
        part = wout_quarter(source, line)
        return remote(part, part, u_s.at[d - 1, to], u_r.at[source, line], at_line[to])

    def quarter_arrival(d, place):
        source = (seq + d) % 4
        part = wout_quarter(source, place)
        return remote(part, part, u_s.at[0, 0], u_r.at[source, place], at_line[0])

    wout_out = [wout_copy(direction) for direction in range(2)]
    wout_pass = [wout_forward(direction, (seq + (3 if direction == 0 else 1)) % 4) for direction in range(2)]
    quarter_out = [quarter_copy(seq, d) for d in (2, 1, 3)]
    quarter_on = [[quarter_pass(d, to) for to in range(3)] for d in (1, 3, 2)]

    def wout_send():
        loads[6].wait()
        for copy in quarter_out + wout_out:
            copy.start()

    def quarter_serve():
        for d, copies in zip((1, 3, 2), quarter_on):
            quarter_copy((seq + d) % 4, 1).wait_recv()
            for copy in copies:
                copy.start()

    def wout_serve():
        for direction in range(2):
            wout_arrival(direction).wait_recv()
            wout_pass[direction].start()

    def wout_last():
        for direction in range(2):
            wout_forward(direction, (seq + 2) % 4).wait_recv()
        for d in (1, 3, 2):
            for place in line_of:
                quarter_arrival(d, place).wait_recv()

    def mod_last():
        for direction in range(2):
            mod_forward(direction).wait_recv()

    start_mod()
    loads[3].wait()
    project(0)
    for load in [loads[4]] + loads[7:]:
        load.wait()
    prompt_rows()
    steps(0)
    mod_arrived(0)
    each_stale(late, lambda copy: copy.start())
    project(1)
    steps(1)
    mod_arrived(1)
    project(2)
    steps(2)
    mod_last()
    prompt_send()
    project(3)
    wout_send()
    for index in range(8):
        attend_next(index)
        if index == 1:
            prompt_project()
        if index == 4:
            prompt_pass()
        if index == 5:
            quarter_serve()
            wout_serve()
        if index == 6:
            prompt_attend()

    guide = guide_in[0]
    first_side = cfg == 0
    mix_out = []
    for h in range(heads):
        lanes = pl.ds(h * HEAD, HEAD)
        att_out[h].wait_recv()
        mine, other = att[h], peer[h]
        cond_part = jnp.where(first_side, mine, other)
        uncond = jnp.where(first_side, other, mine)
        mixed = (uncond + guide * (cond_part - uncond)).astype(BF16)
        mix[:, :, :, lanes] = mixed.reshape(4, 2, 64, HEAD)
        for d, half, group, part in (
            (2, 0, 3, 0), (2, 1, 3, 1), (1, 0, 2, 1), (1, 1, 1, 1), (3, 0, 1, 0), (3, 1, 2, 0),
        ):
            copy = remote(
                mix.at[group, part, :, lanes], mixall.at[seq, half, :, lanes],
                x_s.at[h, d - 1, half], x_r.at[h, seq, half], at_seq(d),
            )
            copy.start()
            mix_out.append(copy)
    total = jnp.dot(mix[0].reshape(128, width), wout[seq], preferred_element_type=F32)
    wout_last()
    for d in (1, 3, 2):
        c = (seq + d) % 4
        for h in range(heads):
            for half in range(2):
                here = mixall.at[c, half, :, pl.ds(h * HEAD, HEAD)]
                remote(here, here, x_s.at[0, 0, 0], x_r.at[h, c, half], at_seq(1)).wait_recv()
        total = total + jnp.dot(mixall[c].reshape(128, width), wout[c], preferred_element_type=F32)
    out_ref[...] = (table[2, pl.ds(now, 1), half_cols] * total).astype(BF16)

    for copy in sum(quarter_on, quarter_out) + mod_out[0] + mod_out[1] + pkv_out + wout_out + wout_pass + att_out + mix_out:
        copy.wait_send()
    @pl.when(lower)
    def _():
        for copy in [pkv_up] + prompt_out:
            copy.wait_send()

    for direction in range(2):
        mod_forward(direction).wait_send()
    each_stale(early, lambda copy: copy.wait_send())
    each_stale(late, lambda copy: copy.wait_send())
    for k in range(4):
        for condition, lane in ((pipe != 7, 0), (pipe != 0, 1), (pipe >= 0, 2)):
            pl.when(condition)(piece(sbuf.at[k], pipe, k, lane, at_x(1)).wait_send)
    for place in range(8):
        @pl.when(pipe == place)
        def _():
            for k in range(4):
                for whence in range(5):
                    for copy in passed(place, whence, k):
                        copy.wait_send()


def local(
    image_states, prompt_states, stale_kv, w_image_qkv, w_prompt_kv, w_output, mod_table, timestep, guidance
):
    rows, model = image_states.shape[1:]
    table = jnp.transpose(mod_table, (1, 0, 2))
    width = w_output.shape[0]
    heads = width // HEAD
    half = w_output.shape[1] // 2
    dma = pltpu.SemaphoreType.DMA
    anywhere = pl.BlockSpec(memory_space=pl.ANY)
    scalar = pl.BlockSpec(memory_space=pltpu.SMEM)
    return pl.pallas_call(
        kernel,
        out_shape=jax.ShapeDtypeStruct((rows, half), BF16),
        in_specs=[anywhere] * 7 + [scalar] * 2,
        out_specs=pl.BlockSpec(memory_space=pltpu.VMEM),
        scratch_shapes=[
            pltpu.VMEM((rows, model), BF16),
            pltpu.VMEM(table.shape, F32),
            pltpu.VMEM((16, model), BF16),
            pltpu.VMEM(w_image_qkv.shape, BF16),
            pltpu.VMEM(w_prompt_kv.shape, BF16),
            pltpu.VMEM((4, width, half), BF16),
            pltpu.VMEM((4, rows, model), BF16),
            pltpu.VMEM((4, 16, model), BF16),
            pltpu.VMEM((4, 2, 64, width), BF16),
            pltpu.VMEM((4, 2, rows, width), BF16),
            pltpu.VMEM((8, 4, 2, rows, width), BF16),
            pltpu.VMEM((heads, 4 * rows, HEAD), BF16),
            pltpu.VMEM((heads, 4 * rows, 2 * HEAD), F32),
            pltpu.VMEM((heads, 4 * rows, HEAD), F32),
            pltpu.VMEM((heads, 4 * rows, HEAD), F32),
            pltpu.VMEM((heads, 4 * rows, HEAD), F32),
            pltpu.VMEM((4, 2, rows // 2, width), BF16),
            pltpu.VMEM((4, 2, rows // 2, width), BF16),
            dma((10,)), dma((3, 4)), dma((4, 4)), dma((2, 2)), dma((2, 2)), dma((2,)), dma((2,)),
            dma((3,)), dma((4,)), dma((4,)), dma((4,)), dma((2,)), dma((2,)), dma((2,)), dma((2,)),
            dma((18, 4)), dma((8, 4)), dma((3,)), dma((4,)), dma((3, 3)), dma((4, 4)), dma((heads,)), dma((heads,)), dma((heads, 3, 2)), dma((heads, 4, 2)),
        ],
        compiler_params=pltpu.CompilerParams(
            collective_id=0, has_side_effects=True, vmem_limit_bytes=58 * 2**20
        ),
        name="guided_attention",
    )(image_states, prompt_states, stale_kv, w_image_qkv, w_prompt_kv, w_output, table, timestep, guidance)


def solution(mesh):
    return jax.shard_map(
        local,
        mesh=mesh,
        in_specs=(
            P("cfg", ("dp", "pipe", "seq"), None),
            P("cfg", ("dp", "seq"), None),
            P("cfg", None, ("dp", "pipe", "seq"), None),
            P(None, None, "seq"),
            P(None, None, "seq"),
            P("seq", None),
            P(),
            P("dp"),
            P("dp"),
        ),
        out_specs=P(("dp", "pipe", "seq"), "cfg"),
        check_vma=False,
    )
```

```python
import math

import jax
import jax.numpy as jnp
from jax import lax
from jax.experimental import pallas as pl
from jax.experimental.pallas import tpu as pltpu
from jax.sharding import PartitionSpec as P

MESH = pl.DeviceIdType.MESH
HEAD = 128
BF16 = jnp.bfloat16
F32 = jnp.float32


PLAN = (
    ((), (17, 1, 18), (9, 16), (12, 19), (), (8, 14, 10, 13, 11), (3,), (), (), (15,), ()),
    ((20, 0, 4, 16, 5, 17), (1, 18, 21), (15, 14), (), (22, 2, 23, 3), (6, 19), (), (7,), (), (), ()),
    ((20, 21, 0, 17, 4), (12, 6, 19), (1, 13), (15,), (22, 16, 2, 23, 18, 14, 3), (), (), (), (), (), ()),
    ((21, 20, 22, 0, 17), (13, 9, 1, 16, 18), (19, 2, 14), (), (23, 12), (3, 15), (), (8,), (), (), ()),
    ((21, 22, 4, 16, 20, 23, 17), (6, 5), (18, 9, 19), (8, 12), (), (10, 7), (13,), (11,), (), (), ()),
    ((20, 21, 22, 0, 5), (8, 7, 6, 16), (9, 18), (), (23, 17, 4), (2, 19), (), (10,), (11,), (), ()),
    ((21, 0, 4, 23, 22, 16, 5), (7, 20, 17, 1), (6, 18, 2), (), (), (19, 3), (), (10, 11), (), (), ()),
    ((20, 21, 22, 23, 12, 8), (16, 13, 17), (9, 18), (), (10, 14, 5, 19, 15), (), (), (11, 7), (), (), ()),
)
ATTEND = (
    (0, 4, 7, 3, 1, 6, 5, 2),
    (1, 0, 5, 4, 2, 6, 3, 7),
    (2, 6, 7, 1, 3, 0, 4, 5),
    (3, 7, 2, 4, 6, 0, 1, 5),
    (4, 0, 5, 7, 3, 6, 2, 1),
    (5, 6, 1, 4, 7, 0, 2, 3),
    (6, 7, 2, 5, 1, 3, 4, 0),
    (7, 3, 6, 0, 5, 2, 4, 1),
)
EARLY = (0, 2, 2, 3, 4, 3, 4, 4)

def passes_to(place, whence, k):
    upper, x = divmod(place, 4)
    if not upper:
        x = 3 - x
        whence = (1, 0, 3, 2, 4)[whence]
    far, near = k in (2, 3), k in (0, 1, 2, 3)
    ways = {
        0: "+" if x == 2 or (x == 1 and k % 2 == 0) or (x == 0 and not near) else "",
        1: ("-" if x == 1 or (x == 2 and near) or (x == 3 and k % 2 == 1) else "") + ("z" if x < 3 else ""),
        2: "+" if x != 2 or far else "",
        3: ("-" if x == 0 and not far else "") + ("z" if x == 3 else ""),
        4: "+-" if x == 3 else "-",
    }[whence]
    return ways if upper else ways.translate(str.maketrans("+-", "-+"))


def patch_from(place, whence):
    upper, x = divmod(place, 4)
    d = (3, 1, 3, 1, 0)[whence]
    return (upper if whence < 2 else 1 - upper) * 4 + (x + d) % 4


def awaited(place, patch, k):
    return any(patch_from(place, w) == patch and passes_to(place, w, k) for w in range(5))


def normalized(rows):
    center = rows - jnp.mean(rows, axis=-1, keepdims=True)
    spread = jnp.mean(center * center, axis=-1, keepdims=True)
    return center * lax.rsqrt(spread + 1e-06)


def kernel(
    img_in, prm_in, stale_in, wqkv_in, wpr_in, wout_in, table_in, step_in, guide_in,
    out_ref,
    img, table, prm, wqkv, wpr, wout, modbuf, prb, pkv, sbuf, kv, q, acc, top, att, peer, mix, mixall,
    lsem, st_s, st_r, m_s, m_r, mf_s, mf_r, pr_s, pr_r, pk_s, pk_r, w_s, w_r, wf_s, wf_r, ss, rs, v_s, v_r, u_s, u_r,
    a_s, a_r, x_s, x_r,
):
    dp, cfg, pipe, seq = (lax.axis_index(name) for name in ("dp", "cfg", "pipe", "seq"))
    x, zh = pipe % 4, pipe // 4
    heads, width = q.shape[0], kv.shape[-1]
    out_half = wout.shape[-1]
    model = img.shape[-1]
    scale = math.log2(math.e) / math.sqrt(HEAD)

    def at_seq(d):
        return (dp, cfg, pipe, (seq + d) % 4)

    def at_x(d):
        return (dp, cfg, zh * 4 + (x + d) % 4, seq)

    at_z = (dp, cfg, (1 - zh) * 4 + x, seq)
    at_core = (dp, 1 - cfg, pipe, seq)
    line = zh * 2 + dp
    at_line = [(1 - dp, cfg, pipe, seq), at_z, (1 - dp, cfg, (1 - zh) * 4 + x, seq)]
    line_of = [zh * 2 + 1 - dp, (1 - zh) * 2 + dp, (1 - zh) * 2 + 1 - dp]

    def remote(src, dst, s, r, device):
        return pltpu.make_async_remote_copy(
            src_ref=src, dst_ref=dst, send_sem=s, recv_sem=r, device_id=device, device_id_type=MESH
        )

    barrier = pltpu.get_barrier_semaphore()
    partners = [at_seq(1), at_seq(3), at_seq(2), at_x(1), at_x(3), at_x(2), at_core] + at_line
    for device in partners:
        pl.semaphore_signal(barrier, inc=1, device_id=device, device_id_type=MESH)

    half_cols = pl.ds(pl.multiple_of(cfg * out_half, 128), out_half)

    def seq_cols(d):
        return pl.ds(pl.multiple_of((seq + d) % 4 * width, 128), width)

    def stale_part(k, source):
        return sbuf.at[k, :, pl.ds(pl.multiple_of(source * 32, 32), 32)]

    loads = [
        pltpu.make_async_copy(img_in.at[0], img, lsem.at[0]),
        pltpu.make_async_copy(table_in, table, lsem.at[1]),
        pltpu.make_async_copy(prm_in.at[0, pl.ds(pl.multiple_of(x * 16, 16), 16)], prm, lsem.at[2]),
        pltpu.make_async_copy(wqkv_in, wqkv, lsem.at[3]),
        pltpu.make_async_copy(stale_in.at[0, :, pl.ds(0, 32), seq_cols(0)], stale_part(0, seq), lsem.at[4]),
        pltpu.make_async_copy(wpr_in, wpr, lsem.at[5]),
        pltpu.make_async_copy(wout_in.at[:, half_cols], wout.at[seq], lsem.at[6]),
    ] + [
        pltpu.make_async_copy(
            stale_in.at[0, :, pl.ds(k * 32, 32), seq_cols(0)], stale_part(k, seq), lsem.at[6 + k]
        )
        for k in (1, 2, 3)
    ]
    for load in loads:
        load.start()

    now = step_in[0]
    loads[0].wait()
    loads[1].wait()

    def modulate(first, count):
        def rows16(i, carry):
            rows = pl.ds(pl.multiple_of(first + i * 16, 16), 16)
            shift, gain = table[0, pl.ds(now, 1), :], table[1, pl.ds(now, 1), :]
            values = normalized(img[rows, :].astype(F32)) * (1.0 + gain) + shift
            modbuf[0, rows, :] = values.astype(BF16)
            return carry

        lax.fori_loop(0, count // 16, rows16, 0)

    modulate(0, 64)
    pl.semaphore_wait(barrier, len(partners))

    def any_of(places):
        found = pipe == places[0]
        for place in places[1:]:
            found = found | (pipe == place)
        return found

    def stale_copy(k, d, source):
        return remote(
            stale_in.at[0, :, pl.ds(k * 32, 32), seq_cols(d)], stale_part(k, source),
            st_s.at[d - 1, k], st_r.at[source, k], at_seq(d),
        )

    stale_out = [[stale_copy(k, d, seq) for d in (2, 1, 3)] for k in range(4)]
    early = [[place for place in range(1, 8) if EARLY[place] > k] for k in range(4)]
    late = [[place for place in range(1, 8) if EARLY[place] <= k] for k in range(4)]

    def each_stale(places, act):
        for k in range(4):
            if places[k]:
                @pl.when(any_of(places[k]))
                def _():
                    for copy in stale_out[k]:
                        act(copy)

    each_stale(early, lambda copy: copy.start())
    modulate(64, 64)

    def half_rows(half):
        return pl.ds(half * 64, 64)

    def mod_copy(direction, order):
        half = direction if order == 0 else 1 - direction
        source = modbuf.at[0, half_rows(half)]
        target = modbuf.at[1 + order, half_rows(direction)]
        return remote(
            source, target, m_s.at[direction, order], m_r.at[direction, order], at_seq(1 if direction == 0 else 3)
        )

    def mod_forward(direction):
        source = modbuf.at[1, half_rows(direction)]
        target = modbuf.at[3, half_rows(direction)]
        return remote(source, target, mf_s.at[direction], mf_r.at[direction], at_seq(1 if direction == 0 else 3))

    mod_out = [[mod_copy(a, b) for b in range(2)] for a in range(2)]

    def piece(source, slot, k, lane, device):
        return remote(source, kv.at[slot, k], ss.at[lane, k], rs.at[slot, k], device)

    att_out = [remote(att.at[h], peer.at[h], a_s.at[h], a_r.at[h], at_core) for h in range(heads)]

    def send_attended(h):
        block = acc[h]
        att[h] = block[:, :HEAD] / block[:, HEAD : HEAD + 1]
        att_out[h].start()

    def toward(way):
        return {"+": at_x(1), "-": at_x(3), "z": at_z}[way]

    def send_own(k):
        for condition, lane, way in ((x < 3, 0, "+"), (pipe == 4, 1, "-"), (zh == 0, 2, "z")):
            pl.when(condition)(piece(kv.at[pipe, k], pipe, k, lane, toward(way)).start)

    def send_stale(place, k):
        upper, column = divmod(place, 4)
        for d in (1, 3, 2):
            stale_copy(k, d, (seq + d) % 4).wait_recv()
        ways = (("+", 0),) * (place == 3) + (("-", 1),) * (column > 0) + (("z", 2),) * upper
        for way, lane in ways:
            piece(sbuf.at[k], place, k, lane, toward(way)).start()

    def landed(slot, k):
        here = kv.at[slot, k]
        remote(here, here, ss.at[0, 0], rs.at[slot, k], at_x(1)).wait_recv()

    def passed(place, whence, k):
        slot = patch_from(place, whence)
        for way in passes_to(place, whence, k):
            yield piece(kv.at[slot, k], slot, k, 3 + 3 * whence + "+-z".index(way), toward(way))

    def step(place, code):
        whence, k = divmod(code, 4)
        if whence == 5:
            send_stale(place, k)
            return
        landed(patch_from(place, whence), k)
        for copy in passed(place, whence, k):
            copy.start()

    def steps(index):
        for place in range(8):
            if PLAN[place][index]:
                @pl.when(pipe == place)
                def _():
                    for code in PLAN[place][index]:
                        step(place, code)

    def attend_next(index):
        steps(3 + index)
        slot = 0
        for place in range(8):
            patch = ATTEND[place][index]
            slot = slot + jnp.where(pipe == place, patch, 0)
            rest = [k for k in range(4) if patch != place and not awaited(place, patch, k)]
            if rest:
                @pl.when(pipe == place)
                def _():
                    for k in rest:
                        landed(patch, k)
        attend_slot(slot, index == 0, send_attended if index == 7 else None)

    def project(k):
        rows = modbuf[k]
        for j in (1, 2):
            kv[pipe, k, j - 1] = jnp.dot(rows, wqkv[j], preferred_element_type=F32).astype(BF16)
        send_own(k)
        block = jnp.dot(rows, wqkv[0], preferred_element_type=F32).astype(BF16)
        for h in range(heads):
            q[h, k * 128 : (k + 1) * 128, :] = block[:, h * HEAD : (h + 1) * HEAD]

    def late_in(k):
        when(x > 0, serve, 0, k)
        when(x == 3, serve, 1, k)

    def late_far(k):
        when(upper, serve, 4, k)

    def late_far_two(k):
        when(upper, serve, 2, k)
        when(upper, serve, 3, k)

    def early_in(k):
        when(x == 0, serve, 0, k)
        when(x < 3, serve, 1, k)

    def early_far(k):
        when(zh == 0, serve, 4, k)

    def early_far_two(k):
        when(zh == 0, serve, 2, k)
        when(zh == 0, serve, 3, k)

    def mod_arrived(order):
        for direction in range(2):
            mod_out[direction][order].wait_recv()
            if order == 0:
                mod_forward(direction).start()

    def attend_head(h, keys, values, first):
        values = jnp.concatenate([values, jnp.ones_like(values)], axis=1)
        scores = lax.dot_general(q[h], keys, (((1,), (1,)), ((), ())), preferred_element_type=F32)
        peak = jnp.max(scores, axis=1, keepdims=True)
        if first:
            new_top = peak
        else:
            old_top = top[h][:, :1]
            new_top = jnp.maximum(old_top, peak)
        weights = jnp.exp2(scores * scale - new_top * scale).astype(BF16)
        part = jnp.dot(weights, values, preferred_element_type=F32)
        if first:
            acc[h] = part
        else:
            acc[h] = acc[h] * jnp.exp2((old_top - new_top) * scale) + part
        top[h] = jnp.broadcast_to(new_top, top.shape[1:])

    def attend(keys_of, values_of, first, finish=None):
        for h in range(heads):
            lanes = pl.ds(h * HEAD, HEAD)
            attend_head(h, keys_of(lanes), values_of(lanes), first)
            if finish is not None:
                finish(h)


    def attend_slot(slot, first=False, finish=None):
        attend(
            lambda lanes: kv[slot, :, 0, :, lanes].reshape(512, HEAD),
            lambda lanes: kv[slot, :, 1, :, lanes].reshape(512, HEAD),
            first,
            finish,
        )

    def start_mod():
        for order in range(2):
            for direction in range(2):
                mod_out[direction][order].start()

    prompt_out = [
        remote(prb.at[seq], prb.at[seq], pr_s.at[d - 1], pr_r.at[seq], at_seq(d)) for d in (1, 3, 2)
    ]
    pkv_up = remote(pkv.at[x], pkv.at[x], pk_s.at[3], pk_r.at[x], at_z)
    pkv_out = [remote(pkv.at[x], pkv.at[x], pk_s.at[d - 1], pk_r.at[x], at_x(d)) for d in (1, 3, 2)]

    lower, upper = zh == 0, zh == 1

    def prompt_rows():
        loads[2].wait()

        @pl.when(lower)
        def _():
            prb[seq] = normalized(prm[...].astype(F32)).astype(BF16)

    def prompt_send():
        @pl.when(lower)
        def _():
            for copy in prompt_out:
                copy.start()

    def prompt_project():
        loads[5].wait()

        @pl.when(lower)
        def _():
            for d in (1, 3, 2):
                c = (seq + d) % 4
                remote(prb.at[c], prb.at[c], pr_s.at[0], pr_r.at[c], at_seq(1)).wait_recv()
            rows = prb[...].reshape(64, model)
            for j in range(2):
                pkv[x, j] = jnp.dot(rows, wpr[j], preferred_element_type=F32).astype(BF16)
            for copy in [pkv_up] + pkv_out:
                copy.start()

    def prompt_pass():
        @pl.when(upper)
        def _():
            pkv_up.wait_recv()
            for copy in pkv_out:
                copy.start()

    def prompt_attend():
        for d in (1, 3, 2):
            c = (x + d) % 4
            remote(pkv.at[c], pkv.at[c], pk_s.at[0], pk_r.at[c], at_x(1)).wait_recv()
        attend(
            lambda lanes: pkv[:, 0, :, lanes].reshape(256, HEAD),
            lambda lanes: pkv[:, 1, :, lanes].reshape(256, HEAD),
            False,
        )

    share = out_half // 3
    quarter = width // 4

    def wout_copy(direction):
        part = wout.at[seq, :, pl.ds(0, out_half - share)]
        return remote(part, part, w_s.at[direction], w_r.at[direction], at_seq(1 if direction == 0 else 3))

    def wout_arrival(direction):
        part = wout.at[(seq + (3 if direction == 0 else 1)) % 4, :, pl.ds(0, out_half - share)]
        return remote(part, part, w_s.at[direction], w_r.at[direction], at_seq(1))

    def wout_forward(direction, source):
        part = wout.at[source, pl.ds(direction * (width // 2), width // 2), pl.ds(0, out_half - share)]
        return remote(part, part, wf_s.at[direction], wf_r.at[direction], at_seq(1 if direction == 0 else 3))

    def wout_quarter(source, place):
        rows = pl.ds(pl.multiple_of(place * quarter, 16), quarter)
        return wout.at[source, rows, pl.ds(out_half - share, share)]

    def quarter_copy(source, d):
        part = wout_quarter(source, line)
        return remote(part, part, v_s.at[d - 1], v_r.at[source], at_seq(d))

    def quarter_pass(d, to):
        source = (seq + d) % 4
        part = wout_quarter(source, line)
        return remote(part, part, u_s.at[d - 1, to], u_r.at[source, line], at_line[to])

    def quarter_arrival(d, place):
        source = (seq + d) % 4
        part = wout_quarter(source, place)
        return remote(part, part, u_s.at[0, 0], u_r.at[source, place], at_line[0])

    wout_out = [wout_copy(direction) for direction in range(2)]
    wout_pass = [wout_forward(direction, (seq + (3 if direction == 0 else 1)) % 4) for direction in range(2)]
    quarter_out = [quarter_copy(seq, d) for d in (2, 1, 3)]
    quarter_on = [[quarter_pass(d, to) for to in range(3)] for d in (1, 3, 2)]

    def wout_send():
        loads[6].wait()
        for copy in quarter_out + wout_out:
            copy.start()

    def quarter_serve():
        for d, copies in zip((1, 3, 2), quarter_on):
            quarter_copy((seq + d) % 4, 1).wait_recv()
            for copy in copies:
                copy.start()

    def wout_serve():
        for direction in range(2):
            wout_arrival(direction).wait_recv()
            wout_pass[direction].start()

    def wout_last(d):
        if d == 2:
            for direction in range(2):
                wout_forward(direction, (seq + 2) % 4).wait_recv()
        for place in line_of:
            quarter_arrival(d, place).wait_recv()

    def mod_last():
        for direction in range(2):
            mod_forward(direction).wait_recv()

    start_mod()
    loads[3].wait()
    project(0)
    for load in [loads[4]] + loads[7:]:
        load.wait()
    prompt_rows()
    steps(0)
    mod_arrived(0)
    each_stale(late, lambda copy: copy.start())
    project(1)
    steps(1)
    mod_arrived(1)
    project(2)
    steps(2)
    mod_last()
    prompt_send()
    project(3)
    wout_send()
    for index in range(8):
        attend_next(index)
        if index == 1:
            prompt_project()
        if index == 4:
            prompt_pass()
        if index == 5:
            quarter_serve()
            wout_serve()
        if index == 6:
            prompt_attend()

    guide = guide_in[0]
    first_side = cfg == 0
    mix_out = []
    for h in range(heads):
        lanes = pl.ds(h * HEAD, HEAD)
        att_out[h].wait_recv()
        mine, other = att[h], peer[h]
        cond_part = jnp.where(first_side, mine, other)
        uncond = jnp.where(first_side, other, mine)
        mixed = (uncond + guide * (cond_part - uncond)).astype(BF16)
        mix[:, :, :, lanes] = mixed.reshape(4, 2, 64, HEAD)
        for d, half, group, part in (
            (2, 0, 3, 0), (2, 1, 3, 1), (1, 0, 2, 1), (1, 1, 1, 1), (3, 0, 1, 0), (3, 1, 2, 0),
        ):
            copy = remote(
                mix.at[group, part, :, lanes], mixall.at[seq, half, :, lanes],
                x_s.at[h, d - 1, half], x_r.at[h, seq, half], at_seq(d),
            )
            copy.start()
            mix_out.append(copy)
    total = jnp.dot(mix[0].reshape(128, width), wout[seq], preferred_element_type=F32)
    for d in (1, 3, 2):
        wout_last(d)
        c = (seq + d) % 4
        for h in range(heads):
            for half in range(2):
                here = mixall.at[c, half, :, pl.ds(h * HEAD, HEAD)]
                remote(here, here, x_s.at[0, 0, 0], x_r.at[h, c, half], at_seq(1)).wait_recv()
        total = total + jnp.dot(mixall[c].reshape(128, width), wout[c], preferred_element_type=F32)
    out_ref[...] = (table[2, pl.ds(now, 1), half_cols] * total).astype(BF16)

    for copy in sum(quarter_on, quarter_out) + mod_out[0] + mod_out[1] + pkv_out + wout_out + wout_pass + att_out + mix_out:
        copy.wait_send()
    @pl.when(lower)
    def _():
        for copy in [pkv_up] + prompt_out:
            copy.wait_send()

    for direction in range(2):
        mod_forward(direction).wait_send()
    each_stale(early, lambda copy: copy.wait_send())
    each_stale(late, lambda copy: copy.wait_send())
    for k in range(4):
        for condition, lane in ((pipe != 7, 0), (pipe != 0, 1), (pipe >= 0, 2)):
            pl.when(condition)(piece(sbuf.at[k], pipe, k, lane, at_x(1)).wait_send)
    for place in range(8):
        @pl.when(pipe == place)
        def _():
            for k in range(4):
                for whence in range(5):
                    for copy in passed(place, whence, k):
                        copy.wait_send()


def local(
    image_states, prompt_states, stale_kv, w_image_qkv, w_prompt_kv, w_output, mod_table, timestep, guidance
):
    rows, model = image_states.shape[1:]
    table = jnp.transpose(mod_table, (1, 0, 2))
    width = w_output.shape[0]
    heads = width // HEAD
    half = w_output.shape[1] // 2
    dma = pltpu.SemaphoreType.DMA
    anywhere = pl.BlockSpec(memory_space=pl.ANY)
    scalar = pl.BlockSpec(memory_space=pltpu.SMEM)
    return pl.pallas_call(
        kernel,
        out_shape=jax.ShapeDtypeStruct((rows, half), BF16),
        in_specs=[anywhere] * 7 + [scalar] * 2,
        out_specs=pl.BlockSpec(memory_space=pltpu.VMEM),
        scratch_shapes=[
            pltpu.VMEM((rows, model), BF16),
            pltpu.VMEM(table.shape, F32),
            pltpu.VMEM((16, model), BF16),
            pltpu.VMEM(w_image_qkv.shape, BF16),
            pltpu.VMEM(w_prompt_kv.shape, BF16),
            pltpu.VMEM((4, width, half), BF16),
            pltpu.VMEM((4, rows, model), BF16),
            pltpu.VMEM((4, 16, model), BF16),
            pltpu.VMEM((4, 2, 64, width), BF16),
            pltpu.VMEM((4, 2, rows, width), BF16),
            pltpu.VMEM((8, 4, 2, rows, width), BF16),
            pltpu.VMEM((heads, 4 * rows, HEAD), BF16),
            pltpu.VMEM((heads, 4 * rows, 2 * HEAD), F32),
            pltpu.VMEM((heads, 4 * rows, HEAD), F32),
            pltpu.VMEM((heads, 4 * rows, HEAD), F32),
            pltpu.VMEM((heads, 4 * rows, HEAD), F32),
            pltpu.VMEM((4, 2, rows // 2, width), BF16),
            pltpu.VMEM((4, 2, rows // 2, width), BF16),
            dma((10,)), dma((3, 4)), dma((4, 4)), dma((2, 2)), dma((2, 2)), dma((2,)), dma((2,)),
            dma((3,)), dma((4,)), dma((4,)), dma((4,)), dma((2,)), dma((2,)), dma((2,)), dma((2,)),
            dma((18, 4)), dma((8, 4)), dma((3,)), dma((4,)), dma((3, 3)), dma((4, 4)), dma((heads,)), dma((heads,)), dma((heads, 3, 2)), dma((heads, 4, 2)),
        ],
        compiler_params=pltpu.CompilerParams(
            collective_id=0, has_side_effects=True, vmem_limit_bytes=58 * 2**20
        ),
        name="guided_attention",
    )(image_states, prompt_states, stale_kv, w_image_qkv, w_prompt_kv, w_output, table, timestep, guidance)


def solution(mesh):
    return jax.shard_map(
        local,
        mesh=mesh,
        in_specs=(
            P("cfg", ("dp", "pipe", "seq"), None),
            P("cfg", ("dp", "seq"), None),
            P("cfg", None, ("dp", "pipe", "seq"), None),
            P(None, None, "seq"),
            P(None, None, "seq"),
            P("seq", None),
            P(),
            P("dp"),
            P("dp"),
        ),
        out_specs=P(("dp", "pipe", "seq"), "cfg"),
        check_vma=False,
    )
```
